32 devices in a mesh: grp: 2 (over y), row: 4 (over z), feat: 4 (over x, core).
Axes of the slice: x: 2, y: 2, z: 4, core: 2. Of those that a mesh axis runs over, the one named last changes fastest.
Arguments:
- queries: float32 [512, 8192], P('row', 'feat'), may hold values from -0.0625 to 0.0625
- train_rows: float32 [832, 8192], P(('grp', 'row'), 'feat'), parts along dimension 0, may hold values from -6 to 6
- inv_gram: float32 [16, 512, 512], P('feat')
Outputs:
- scores: float32 [512, 832], P('row', ('grp', 'feat')), parts along dimension 1
The draws below stay inside these ranges and needn't reach their ends.
There are 2 independent parts, one for each index of `grp`. The reference program is written for one: setup_inputs(seed, part) draws one part's arguments, and reference() takes and returns one part's arrays. A program takes and returns all parts, laid end to end along the dimension named above; an argument that names none is the same for every part. Nothing has to cross between parts.
All inputs are finite; a program needn't handle non-finite values.
Results may differ from the reference program's by a relative error of at most 0.000082.
Values sent between devices are 32-bit elements; how exact they have to be, the bound alone decides.
No kernel may reach another device: no remote copies, remote signals or barrier semaphores. Data moves between devices by JAX's collectives and lax.ppermute only.
A program may use at most 64 MiB of HBM per device.

```python
import jax
import jax.numpy as jnp
from jax import lax

F = 8192
MODULE = 512
NQ = 512
NT = 416


def draw_inv_gram(key, part):
    key = jax.random.fold_in(key, 7)
    key_diag, key_off = jax.random.split(key)
    nblocks = F // MODULE
    diag = jnp.exp(jax.random.uniform(key_diag, (nblocks, MODULE), jnp.float32, jnp.log(0.5), jnp.log(2.0)))
    off = jax.random.normal(key_off, (nblocks, MODULE, MODULE), jnp.float32) * (0.5 / MODULE ** 0.5)
    eye = jnp.eye(MODULE, dtype=jnp.float32)
    return off + eye[None, :, :] * diag[:, :, None]


def level_of(key, shape, cuts, smallest, top_value):
    def one(position, parts):
        heights = jax.random.uniform(jax.random.fold_in(jax.random.fold_in(key, 6), position), (parts,), jnp.float32, smallest / len(cuts), top_value / len(cuts))
        return jnp.repeat(jnp.exp(heights), shape[position] // parts).reshape((-1,) + (1,) * (len(shape) - position - 1))

    factor_of = one(*cuts[0])
    for cut in cuts[1:]:
        factor_of = factor_of * one(*cut)
    return factor_of


def bell_draw(stream_key, shape, scale, most, pieces=(), kind=jnp.bfloat16):
    level = level_of(stream_key, shape, pieces, -0.22, 0.18) if pieces else 1.0
    entries = jax.random.normal(stream_key, shape, jnp.float32) * scale * level
    return jnp.minimum(jnp.maximum(entries, -most), most).astype(kind)


def setup_inputs(seed: int = 0, part: int = 0) -> dict:
    key_list = jax.random.split(jax.random.key(seed), 4)
    part_keys = jax.random.split(jax.random.fold_in(key_list[3], part), 4)
    queries = bell_draw(key_list[0], (NQ, F), F ** -0.5, 0.0625, ((0, 4), (1, 4)), jnp.float32)
    train_rows = bell_draw(part_keys[1], (NT, F), 1.0, 6.0, ((0, 4), (1, 4)), jnp.float32)
    inv_gram = draw_inv_gram(jax.random.fold_in(key_list[3], 71), part)
    return dict(queries=queries, train_rows=train_rows, inv_gram=inv_gram)


def reference(queries, train_rows, inv_gram):
    blocks = queries.reshape(queries.shape[0], F // MODULE, MODULE)
    conditioned = jnp.einsum("qbi,bij->qbj", blocks, inv_gram, precision=lax.Precision.HIGHEST)
    conditioned = conditioned.reshape(queries.shape[0], F)
    return jnp.dot(conditioned, train_rows.T, precision=lax.Precision.HIGHEST, preferred_element_type=jnp.float32)
```

```python
import jax
import jax.numpy as jnp
from jax import lax
from jax.sharding import PartitionSpec as P

HIGHEST = lax.Precision.HIGHEST


def send(array, axis, to):
    devices = lax.axis_size(axis)
    return lax.ppermute(array, axis, [(i, to(i)) for i in range(devices)])


def swap(array, axis, bit):
    return send(array, axis, lambda i: i ^ bit)


def condition(queries, inv_gram):
    rows = queries.shape[0]
    nblocks, modsize = inv_gram.shape[0], inv_gram.shape[1]
    blocks = queries.reshape(rows, nblocks, modsize)
    out = jnp.einsum("qbi,bij->qbj", blocks, inv_gram, precision=HIGHEST)
    return out.reshape(rows, nblocks * modsize)


def block_scores(left, right):
    return jnp.dot(left, right.T, precision=HIGHEST, preferred_element_type=jnp.float32)


def shards(queries, train_rows, inv_gram):
    qrows, fshard = queries.shape
    trows = train_rows.shape[0]
    nrow, nfeat = lax.axis_size("row"), lax.axis_size("feat")
    row, feat = lax.axis_index("row"), lax.axis_index("feat")
    half, nmod = fshard // 2, inv_gram.shape[0] // 2
    side = row % 2

    def mine(array):
        return lax.dynamic_slice_in_dim(array, side * half, half, 1)

    def others(array):
        return lax.dynamic_slice_in_dim(array, (1 - side) * half, half, 1)

    q_mine, q_others = mine(queries), others(queries)
    t_mine, t_others = mine(train_rows), others(train_rows)
    q_pair = swap(q_others, "row", 1)
    blocks = [(t_mine, row), (swap(t_others, "row", 1), row ^ 1)]
    for step in range(2, nrow, 2):
        blocks.append((send(t_mine, "row", lambda i: (i + step) % nrow), (row - step) % nrow))
        blocks.append((send(t_others, "row", lambda i: ((i + step) % nrow) ^ 1), ((row ^ 1) - step) % nrow))

    gram = lax.dynamic_slice_in_dim(inv_gram, side * nmod, nmod, 0)
    conditioned = condition(jnp.concatenate([q_mine, q_pair], axis=0), gram)
    partial = jnp.zeros((nrow, 2 * qrows, trows), jnp.float32)
    for block, source in blocks:
        partial = lax.dynamic_update_slice(partial, block_scores(conditioned, block)[None], (source, 0, 0))

    left, bit = nfeat, 1
    partial = partial.reshape(nfeat, nrow // nfeat, 2 * qrows, trows)
    while left > 1:
        pairs = partial.reshape(left // 2, 2, *partial.shape[1:])
        odd = (feat // bit) % 2 == 1
        keep = jnp.where(odd, pairs[:, 1], pairs[:, 0])
        give = jnp.where(odd, pairs[:, 0], pairs[:, 1])
        partial = keep + swap(give, "feat", bit)
        left, bit = left // 2, bit * 2
    partial = partial[0]
    scores = partial[:, :qrows] + swap(partial[:, qrows:], "row", 1)
    return scores.transpose(1, 0, 2).reshape(qrows, -1)


def solution(mesh):
    return jax.shard_map(
        shards,
        mesh=mesh,
        in_specs=(P("row", "feat"), P(("grp", "row"), "feat"), P("feat", None, None)),
        out_specs=P("row", ("grp", "feat")),
        check_vma=False,
    )
```

```python
import functools

import jax
import jax.numpy as jnp
from jax import lax
from jax.experimental import pallas as pl
from jax.experimental.pallas import tpu as pltpu
from jax.sharding import PartitionSpec as P

HIGHEST = lax.Precision.HIGHEST
ANYWHERE = pl.BlockSpec(memory_space=pl.ANY)
VMEM = pl.BlockSpec(memory_space=pltpu.VMEM)
FREE = pl.CostEstimate(flops=0, bytes_accessed=0, transcendentals=0)


def send(array, axis, to):
    devices = lax.axis_size(axis)
    return lax.ppermute(array, axis, [(i, to(i)) for i in range(devices)])


def swap(array, axis, bit):
    return send(array, axis, lambda i: i ^ bit)


def condition(queries, inv_gram):
    rows = queries.shape[0]
    nblocks, modsize = inv_gram.shape[0], inv_gram.shape[1]
    blocks = queries.reshape(rows, nblocks, modsize)
    out = jnp.einsum("qbi,bij->qbj", blocks, inv_gram, precision=HIGHEST)
    return out.reshape(rows, nblocks * modsize)


def block_scores(left, right):
    return jnp.dot(left, right.T, precision=HIGHEST, preferred_element_type=jnp.float32)


def any_shards(queries, train_rows, inv_gram):
    qrows, fshard = queries.shape
    trows = train_rows.shape[0]
    nrow, nfeat = lax.axis_size("row"), lax.axis_size("feat")
    row, feat = lax.axis_index("row"), lax.axis_index("feat")
    half, nmod = fshard // 2, inv_gram.shape[0] // 2
    side = row % 2

    def mine(array):
        return lax.dynamic_slice_in_dim(array, side * half, half, 1)

    def others(array):
        return lax.dynamic_slice_in_dim(array, (1 - side) * half, half, 1)

    q_mine, q_others = mine(queries), others(queries)
    t_mine, t_others = mine(train_rows), others(train_rows)
    q_pair = swap(q_others, "row", 1)
    blocks = [(t_mine, row), (swap(t_others, "row", 1), row ^ 1)]
    for step in range(2, nrow, 2):
        blocks.append((send(t_mine, "row", lambda i: (i + step) % nrow), (row - step) % nrow))
        blocks.append((send(t_others, "row", lambda i: ((i + step) % nrow) ^ 1), ((row ^ 1) - step) % nrow))

    gram = lax.dynamic_slice_in_dim(inv_gram, side * nmod, nmod, 0)
    conditioned = condition(jnp.concatenate([q_mine, q_pair], axis=0), gram)
    partial = jnp.zeros((nrow, 2 * qrows, trows), jnp.float32)
    for block, source in blocks:
        partial = lax.dynamic_update_slice(partial, block_scores(conditioned, block)[None], (source, 0, 0))

    left, bit = nfeat, 1
    partial = partial.reshape(nfeat, nrow // nfeat, 2 * qrows, trows)
    while left > 1:
        pairs = partial.reshape(left // 2, 2, *partial.shape[1:])
        odd = (feat // bit) % 2 == 1
        keep = jnp.where(odd, pairs[:, 1], pairs[:, 0])
        give = jnp.where(odd, pairs[:, 0], pairs[:, 1])
        partial = keep + swap(give, "feat", bit)
        left, bit = left // 2, bit * 2
    partial = partial[0]
    scores = partial[:, :qrows] + swap(partial[:, qrows:], "row", 1)
    return scores.transpose(1, 0, 2).reshape(qrows, -1)


def split(x):
    high = x.astype(jnp.bfloat16)
    return high, (x - high.astype(jnp.float32)).astype(jnp.bfloat16)


def condition_kernel(side_ref, q_ref, pair_ref, gram_ref, high_ref, low_ref):
    q_high, q_low = split(jnp.concatenate([q_ref[...], pair_ref[...]], axis=0))
    g_high, g_low = split(gram_ref[0])
    dot = functools.partial(jnp.dot, preferred_element_type=jnp.float32)
    out = dot(q_high, g_low) + dot(q_low, g_high) + dot(q_high, g_high)
    high_ref[...], low_ref[...] = split(out)


def condition_pair(queries, pair, inv_gram, side):
    qrows = queries.shape[0]
    nmod, modsize = inv_gram.shape[0] // 2, inv_gram.shape[1]
    out = jax.ShapeDtypeStruct((2 * qrows, nmod * modsize), jnp.bfloat16)
    return pl.pallas_call(
        condition_kernel,
        out_shape=[out, out],
        grid_spec=pltpu.PrefetchScalarGridSpec(
            num_scalar_prefetch=1,
            grid=(nmod,),
            in_specs=[
                pl.BlockSpec((qrows, modsize), lambda m, side: (0, side[0] * nmod + m)),
                pl.BlockSpec((qrows, modsize), lambda m, side: (0, m)),
                pl.BlockSpec((1, modsize, modsize), lambda m, side: (side[0] * nmod + m, 0, 0)),
            ],
            out_specs=[pl.BlockSpec((2 * qrows, modsize), lambda m, side: (0, m))] * 2,
        ),
        cost_estimate=FREE,
        compiler_params=pltpu.CompilerParams(vmem_limit_bytes=24 << 20),
    )(side.reshape(1), queries, pair, inv_gram)


def scores_kernel(high_ref, low_ref, t_ref, *refs):
    out_ref = refs[-1]
    t_high, t_low = split(t_ref[...])
    dot = functools.partial(
        lax.dot_general, dimension_numbers=(((1,), (1,)), ((), ())), preferred_element_type=jnp.float32
    )
    high, low = high_ref[...], low_ref[...]
    out_ref[...] = dot(high, t_low) + dot(low, t_high) + dot(high, t_high)


def score(conditioned, block, *after):
    high, low = conditioned
    return pl.pallas_call(
        scores_kernel,
        out_shape=jax.ShapeDtypeStruct((high.shape[0], block.shape[0]), jnp.float32),
        in_specs=[VMEM] * 3 + [ANYWHERE] * len(after),
        out_specs=VMEM,
        cost_estimate=FREE,
        compiler_params=pltpu.CompilerParams(vmem_limit_bytes=16 << 20),
    )(high, low, block, *after)


def swap_both(array, row_bit, feat_bit):
    nrow, nfeat = lax.axis_size("row"), lax.axis_size("feat")
    pairs = [
        (r * nfeat + f, (r ^ row_bit) * nfeat + (f ^ feat_bit)) for r in range(nrow) for f in range(nfeat)
    ]
    return lax.ppermute(array, ("row", "feat"), pairs)


def four_shards(queries, train_rows, inv_gram):
    qrows, half = queries.shape[0], queries.shape[1] // 2
    row, feat = lax.axis_index("row"), lax.axis_index("feat")
    side = row % 2
    t_others = lax.dynamic_slice_in_dim(train_rows, (1 - side) * half, half, 1)
    cross = swap(t_others, "row", 3)
    q_others = lax.dynamic_slice_in_dim(queries, (1 - side) * half, half, 1)
    q_pair = swap(q_others, "row", 1)
    t_mine = lax.dynamic_slice_in_dim(train_rows, side * half, half, 1)
    far = swap(t_mine, "row", 2)
    near = swap(t_others, "row", 1)
    conditioned = condition_pair(queries, q_pair, inv_gram, side)

    blocks = [score(conditioned, block) for block in (t_mine, near, far, cross)]
    own, odd = (row ^ feat) % 2 == 0, ((row ^ feat) // 2) % 2 == 1
    give = jnp.stack([jnp.where(own, blocks[1], blocks[0]), jnp.where(own, blocks[3], blocks[2])])
    keep = jnp.stack([jnp.where(own, blocks[0], blocks[1]), jnp.where(own, blocks[2], blocks[3])])
    keep = keep + swap(give, "feat", 1)
    give, keep = jnp.where(odd, keep[0], keep[1]), jnp.where(odd, keep[1], keep[0])
    return (
        keep[:qrows]
        + swap_both(give[:qrows], 0, 2)
        + swap_both(keep[qrows:], 1, 0)
        + swap_both(give[qrows:], 1, 2)
    )


def solution(mesh):
    four = mesh.shape["row"] == 4 and mesh.shape["feat"] == 4
    return jax.shard_map(
        four_shards if four else any_shards,
        mesh=mesh,
        in_specs=(P("row", "feat"), P(("grp", "row"), "feat"), P("feat", None, None)),
        out_specs=P("row", ("grp", "feat")),
        check_vma=False,
    )
```

```python
import functools

import jax
import jax.numpy as jnp
from jax import lax
from jax.experimental import pallas as pl
from jax.experimental.pallas import tpu as pltpu
from jax.sharding import PartitionSpec as P

HIGHEST = lax.Precision.HIGHEST
ANYWHERE = pl.BlockSpec(memory_space=pl.ANY)
VMEM = pl.BlockSpec(memory_space=pltpu.VMEM)
FREE = pl.CostEstimate(flops=0, bytes_accessed=0, transcendentals=0)


def send(array, axis, to):
    devices = lax.axis_size(axis)
    return lax.ppermute(array, axis, [(i, to(i)) for i in range(devices)])


def swap(array, axis, bit):
    return send(array, axis, lambda i: i ^ bit)


def condition(queries, inv_gram):
    rows = queries.shape[0]
    nblocks, modsize = inv_gram.shape[0], inv_gram.shape[1]
    blocks = queries.reshape(rows, nblocks, modsize)
    out = jnp.einsum("qbi,bij->qbj", blocks, inv_gram, precision=HIGHEST)
    return out.reshape(rows, nblocks * modsize)


def block_scores(left, right):
    return jnp.dot(left, right.T, precision=HIGHEST, preferred_element_type=jnp.float32)


def any_shards(queries, train_rows, inv_gram):
    qrows, fshard = queries.shape
    trows = train_rows.shape[0]
    nrow, nfeat = lax.axis_size("row"), lax.axis_size("feat")
    row, feat = lax.axis_index("row"), lax.axis_index("feat")
    half, nmod = fshard // 2, inv_gram.shape[0] // 2
    side = row % 2

    def mine(array):
        return lax.dynamic_slice_in_dim(array, side * half, half, 1)

    def others(array):
        return lax.dynamic_slice_in_dim(array, (1 - side) * half, half, 1)

    q_mine, q_others = mine(queries), others(queries)
    t_mine, t_others = mine(train_rows), others(train_rows)
    q_pair = swap(q_others, "row", 1)
    blocks = [(t_mine, row), (swap(t_others, "row", 1), row ^ 1)]
    for step in range(2, nrow, 2):
        blocks.append((send(t_mine, "row", lambda i: (i + step) % nrow), (row - step) % nrow))
        blocks.append((send(t_others, "row", lambda i: ((i + step) % nrow) ^ 1), ((row ^ 1) - step) % nrow))

    gram = lax.dynamic_slice_in_dim(inv_gram, side * nmod, nmod, 0)
    conditioned = condition(jnp.concatenate([q_mine, q_pair], axis=0), gram)
    partial = jnp.zeros((nrow, 2 * qrows, trows), jnp.float32)
    for block, source in blocks:
        partial = lax.dynamic_update_slice(partial, block_scores(conditioned, block)[None], (source, 0, 0))

    left, bit = nfeat, 1
    partial = partial.reshape(nfeat, nrow // nfeat, 2 * qrows, trows)
    while left > 1:
        pairs = partial.reshape(left // 2, 2, *partial.shape[1:])
        odd = (feat // bit) % 2 == 1
        keep = jnp.where(odd, pairs[:, 1], pairs[:, 0])
        give = jnp.where(odd, pairs[:, 0], pairs[:, 1])
        partial = keep + swap(give, "feat", bit)
        left, bit = left // 2, bit * 2
    partial = partial[0]
    scores = partial[:, :qrows] + swap(partial[:, qrows:], "row", 1)
    return scores.transpose(1, 0, 2).reshape(qrows, -1)


def pack_kernel(q_ref, t_ref, q_others, t_others, t_mine, sems):
    side = lax.axis_index("row") % 2
    half = t_mine.shape[1]
    mine = pl.ds(pl.multiple_of(side * half, half), half)
    others = pl.ds(pl.multiple_of((1 - side) * half, half), half)
    copies = [
        pltpu.make_async_copy(q_ref.at[:, others], q_others, sems.at[0]),
        pltpu.make_async_copy(t_ref.at[:, others], t_others, sems.at[1]),
        pltpu.make_async_copy(t_ref.at[:, mine], t_mine, sems.at[2]),
    ]
    for copy in copies:
        copy.start()
    for copy in copies:
        copy.wait()


def pack(queries, train_rows):
    qrows, half = queries.shape[0], queries.shape[1] // 2
    trows = train_rows.shape[0]
    return pl.pallas_call(
        pack_kernel,
        out_shape=[pltpu.VMEM((rows, half), jnp.float32) for rows in (qrows, trows, trows)],
        in_specs=[ANYWHERE] * 2,
        out_specs=[VMEM] * 3,
        scratch_shapes=[pltpu.SemaphoreType.DMA((3,))],
        cost_estimate=FREE,
    )(queries, train_rows)


def split(x):
    high = x.astype(jnp.bfloat16)
    return high, (x - high.astype(jnp.float32)).astype(jnp.bfloat16)


def condition_kernel(side_ref, q_ref, pair_ref, gram_ref, after_ref, high_ref, low_ref):
    q_high, q_low = split(jnp.concatenate([q_ref[...], pair_ref[...]], axis=0))
    g_high, g_low = split(gram_ref[0])
    dot = functools.partial(jnp.dot, preferred_element_type=jnp.float32)
    out = dot(q_high, g_low) + dot(q_low, g_high) + dot(q_high, g_high)
    high_ref[...], low_ref[...] = split(out)


def condition_pair(queries, pair, inv_gram, side, after):
    qrows = queries.shape[0]
    nmod, modsize = inv_gram.shape[0] // 2, inv_gram.shape[1]
    out = jax.ShapeDtypeStruct((2 * qrows, nmod * modsize), jnp.bfloat16)
    return pl.pallas_call(
        condition_kernel,
        out_shape=[out, out],
        grid_spec=pltpu.PrefetchScalarGridSpec(
            num_scalar_prefetch=1,
            grid=(nmod,),
            in_specs=[
                pl.BlockSpec((qrows, modsize), lambda m, side: (0, side[0] * nmod + m)),
                pl.BlockSpec((qrows, modsize), lambda m, side: (0, m)),
                pl.BlockSpec((1, modsize, modsize), lambda m, side: (side[0] * nmod + m, 0, 0)),
                ANYWHERE,
            ],
            out_specs=[pl.BlockSpec((2 * qrows, modsize), lambda m, side: (0, m))] * 2,
        ),
        cost_estimate=FREE,
        compiler_params=pltpu.CompilerParams(vmem_limit_bytes=24 << 20),
    )(side.reshape(1), queries, pair, inv_gram, after)


def block_scores_of(high, low, t_ref):
    rows = t_ref.shape[0]
    t_high, t_low = split(t_ref[...])
    dot = functools.partial(
        lax.dot_general, dimension_numbers=(((1,), (1,)), ((), ())), preferred_element_type=jnp.float32
    )
    both = dot(jnp.concatenate([t_high, t_low], axis=0), high)
    return both[rows:] + dot(t_high, low) + both[:rows]


def scores_kernel(high_ref, low_ref, t_ref, out_ref):
    out_ref[...] = block_scores_of(high_ref[...], low_ref[...], t_ref)


def score(conditioned, block):
    return pl.pallas_call(
        scores_kernel,
        out_shape=jax.ShapeDtypeStruct((block.shape[0], conditioned[0].shape[0]), jnp.float32),
        in_specs=[VMEM] * 3,
        out_specs=VMEM,
        cost_estimate=FREE,
        compiler_params=pltpu.CompilerParams(vmem_limit_bytes=16 << 20),
    )(*conditioned, block)


def last_kernel(flip_ref, high_ref, low_ref, near_ref, own_ref, far_ref, cross_ref, keep_ref, give_ref):
    near = block_scores_of(high_ref[...], low_ref[...], near_ref)
    own, far, cross = own_ref[...], far_ref[...], cross_ref[...]
    flip = flip_ref[0] != 0
    keep_ref[0], give_ref[0] = jnp.where(flip, near, own), jnp.where(flip, own, near)
    keep_ref[1], give_ref[1] = jnp.where(flip, cross, far), jnp.where(flip, far, cross)


def last_scores(conditioned, near, others, flip):
    out = jax.ShapeDtypeStruct((2, *others[0].shape), jnp.float32)
    return pl.pallas_call(
        last_kernel,
        out_shape=[out, out],
        in_specs=[pl.BlockSpec(memory_space=pltpu.SMEM)] + [VMEM] * 6,
        out_specs=[VMEM] * 2,
        cost_estimate=FREE,
        compiler_params=pltpu.CompilerParams(vmem_limit_bytes=16 << 20),
    )(flip.reshape(1), *conditioned, near, *others)


def swap_both(array, row_bit, feat_bit):
    nrow, nfeat = lax.axis_size("row"), lax.axis_size("feat")
    pairs = [
        (r * nfeat + f, (r ^ row_bit) * nfeat + (f ^ feat_bit)) for r in range(nrow) for f in range(nfeat)
    ]
    return lax.ppermute(array, ("row", "feat"), pairs)


def four_shards(queries, train_rows, inv_gram):
    qrows = queries.shape[0]
    row, feat = lax.axis_index("row"), lax.axis_index("feat")
    side = row % 2
    q_others, t_others, t_mine = pack(queries, train_rows)
    q_pair = swap(q_others, "row", 1)
    cross = swap(t_others, "row", 3)
    far = swap(t_mine, "row", 2)
    near = swap(t_others, "row", 1)
    conditioned = condition_pair(queries, q_pair, inv_gram, side, cross)

    others = [score(conditioned, block) for block in (t_mine, far, cross)]
    flip = (row ^ feat) % 2
    keep, give = last_scores(conditioned, near, others, flip)
    keep = keep + swap(give, "feat", 1)
    odd = ((row ^ feat) // 2) % 2 == 1
    give, keep = jnp.where(odd, keep[0], keep[1]), jnp.where(odd, keep[1], keep[0])
    own, other = slice(0, qrows), slice(qrows, 2 * qrows)
    there = swap_both(keep[:, other], 1, 0)
    across = swap_both(give[:, other], 1, 2)
    beside = swap_both(give[:, own], 0, 2)
    return (keep[:, own] + there + across + beside).T


def solution(mesh):
    four = mesh.shape["row"] == 4 and mesh.shape["feat"] == 4
    return jax.shard_map(
        four_shards if four else any_shards,
        mesh=mesh,
        in_specs=(P("row", "feat"), P(("grp", "row"), "feat"), P("feat", None, None)),
        out_specs=P("row", ("grp", "feat")),
        check_vma=False,
    )
```

```python
import functools

import jax
import jax.numpy as jnp
from jax import lax
from jax.experimental import pallas as pl
from jax.experimental.pallas import tpu as pltpu
from jax.sharding import PartitionSpec as P

HIGHEST = lax.Precision.HIGHEST
ANYWHERE = pl.BlockSpec(memory_space=pl.ANY)
VMEM = pl.BlockSpec(memory_space=pltpu.VMEM)
FREE = pl.CostEstimate(flops=0, bytes_accessed=0, transcendentals=0)


def send(array, axis, to):
    devices = lax.axis_size(axis)
    return lax.ppermute(array, axis, [(i, to(i)) for i in range(devices)])


def swap(array, axis, bit):
    return send(array, axis, lambda i: i ^ bit)


SPLIT_COST = pl.CostEstimate(flops=8589934592, bytes_accessed=67108864, transcendentals=0)
PREPARE_COST = pl.CostEstimate(flops=1 << 31, bytes_accessed=8 << 20, transcendentals=0)


def condition(queries, inv_gram):
    rows = queries.shape[0]
    nblocks, modsize = inv_gram.shape[0], inv_gram.shape[1]
    blocks = queries.reshape(rows, nblocks, modsize)
    out = jnp.einsum("qbi,bij->qbj", blocks, inv_gram, precision=HIGHEST)
    return out.reshape(rows, nblocks * modsize)


def block_scores(left, right):
    return jnp.dot(left, right.T, precision=HIGHEST, preferred_element_type=jnp.float32)


def any_shards(queries, train_rows, inv_gram):
    qrows, fshard = queries.shape
    trows = train_rows.shape[0]
    nrow, nfeat = lax.axis_size("row"), lax.axis_size("feat")
    row, feat = lax.axis_index("row"), lax.axis_index("feat")
    half, nmod = fshard // 2, inv_gram.shape[0] // 2
    side = row % 2

    def mine(array):
        return lax.dynamic_slice_in_dim(array, side * half, half, 1)

    def others(array):
        return lax.dynamic_slice_in_dim(array, (1 - side) * half, half, 1)

    q_mine, q_others = mine(queries), others(queries)
    t_mine, t_others = mine(train_rows), others(train_rows)
    q_pair = swap(q_others, "row", 1)
    blocks = [(t_mine, row), (swap(t_others, "row", 1), row ^ 1)]
    for step in range(2, nrow, 2):
        blocks.append((send(t_mine, "row", lambda i: (i + step) % nrow), (row - step) % nrow))
        blocks.append((send(t_others, "row", lambda i: ((i + step) % nrow) ^ 1), ((row ^ 1) - step) % nrow))

    gram = lax.dynamic_slice_in_dim(inv_gram, side * nmod, nmod, 0)
    conditioned = condition(jnp.concatenate([q_mine, q_pair], axis=0), gram)
    partial = jnp.zeros((nrow, 2 * qrows, trows), jnp.float32)
    for block, source in blocks:
        partial = lax.dynamic_update_slice(partial, block_scores(conditioned, block)[None], (source, 0, 0))

    left, bit = nfeat, 1
    partial = partial.reshape(nfeat, nrow // nfeat, 2 * qrows, trows)
    while left > 1:
        pairs = partial.reshape(left // 2, 2, *partial.shape[1:])
        odd = (feat // bit) % 2 == 1
        keep = jnp.where(odd, pairs[:, 1], pairs[:, 0])
        give = jnp.where(odd, pairs[:, 0], pairs[:, 1])
        partial = keep + swap(give, "feat", bit)
        left, bit = left // 2, bit * 2
    partial = partial[0]
    scores = partial[:, :qrows] + swap(partial[:, qrows:], "row", 1)
    return scores.transpose(1, 0, 2).reshape(qrows, -1)


def pack_kernel(q_ref, t_ref, q_others, t_others, t_mine, sems):
    side = lax.axis_index("row") % 2
    qrows = q_others.shape[0]
    rows = pl.ds(pl.multiple_of(lax.axis_index("grp") * qrows, qrows), qrows)
    half = t_mine.shape[1]
    mine = pl.ds(pl.multiple_of(side * half, half), half)
    others = pl.ds(pl.multiple_of((1 - side) * half, half), half)
    copies = [
        pltpu.make_async_copy(q_ref.at[rows, others], q_others, sems.at[0]),
        pltpu.make_async_copy(t_ref.at[:, others], t_others, sems.at[1]),
        pltpu.make_async_copy(t_ref.at[:, mine], t_mine, sems.at[2]),
    ]
    for copy in copies:
        copy.start()
    for copy in copies:
        copy.wait()


def pack(queries, train_rows):
    qrows, half = queries.shape[0] // 2, queries.shape[1] // 2
    trows = train_rows.shape[0]
    return pl.pallas_call(
        pack_kernel,
        out_shape=[pltpu.VMEM((rows, half), jnp.float32) for rows in (qrows, trows, trows)],
        in_specs=[ANYWHERE] * 2,
        out_specs=[VMEM] * 3,
        scratch_shapes=[pltpu.SemaphoreType.DMA((3,))],
        cost_estimate=FREE,
    )(queries, train_rows)


def split(x):
    high = x.astype(jnp.bfloat16)
    return high, (x - high.astype(jnp.float32)).astype(jnp.bfloat16)


def dot3(left, right, dimension_numbers):
    dot = functools.partial(
        lax.dot_general, dimension_numbers=dimension_numbers, preferred_element_type=jnp.float32
    )
    return dot(left[0], right[1]) + dot(left[1], right[0]) + dot(left[0], right[0])


PLAIN = (((1,), (0,)), ((), ()))


def prepare_kernel(q_hbm, gram_hbm, high_ref, low_ref, g_high_ref, g_low_ref, q_ref, gram_ref, sems):
    side = lax.axis_index("row") % 2
    nmod, modsize = gram_ref.shape[0], gram_ref.shape[1]
    half = nmod * modsize
    get_q = pltpu.make_async_copy(q_hbm.at[:, pl.ds(pl.multiple_of(side * half, half), half)], q_ref, sems.at[0])
    get_gram = pltpu.make_async_copy(gram_hbm.at[pl.ds(side * nmod, nmod)], gram_ref, sems.at[1])
    get_q.start()
    get_gram.start()
    get_q.wait()
    get_gram.wait()
    for m in range(nmod):
        columns = slice(m * modsize, (m + 1) * modsize)
        gram = split(gram_ref[m])
        g_high_ref[m], g_low_ref[m] = gram
        high_ref[:, columns], low_ref[:, columns] = split(dot3(split(q_ref[:, columns]), gram, PLAIN))


def prepare(queries, inv_gram):
    qrows, half = queries.shape[0], queries.shape[1] // 2
    nmod, modsize = inv_gram.shape[0] // 2, inv_gram.shape[1]
    conditioned = pltpu.VMEM((qrows, half), jnp.bfloat16)
    gram = pltpu.VMEM((nmod, modsize, modsize), jnp.bfloat16)
    return pl.pallas_call(
        prepare_kernel,
        out_shape=[conditioned, conditioned, gram, gram],
        in_specs=[ANYWHERE] * 2,
        out_specs=[VMEM] * 4,
        scratch_shapes=[
            pltpu.VMEM((qrows, half), jnp.float32),
            pltpu.VMEM((nmod, modsize, modsize), jnp.float32),
            pltpu.SemaphoreType.DMA((2,)),
        ],
        cost_estimate=PREPARE_COST,
        compiler_params=pltpu.CompilerParams(vmem_limit_bytes=24 << 20),
    )(queries, inv_gram)


def condition_kernel(own_high, own_low, g_high, g_low, straight_ref, swapped_ref, after_ref, high_ref, low_ref):
    qrows, modsize = own_high.shape[0], g_high.shape[1]
    first = lax.axis_index("grp") == 0
    high_ref[:qrows], low_ref[:qrows] = own_high[...], own_low[...]
    for m in range(g_high.shape[0]):
        columns = slice(m * modsize, (m + 1) * modsize)
        straight, swapped = straight_ref[:, columns], swapped_ref[:, columns]
        pair = [jnp.where(first, straight, swapped), jnp.where(first, swapped, straight)]
        out = dot3(split(jnp.concatenate(pair, axis=0)), (g_high[m], g_low[m]), PLAIN)
        high_ref[qrows:, columns], low_ref[qrows:, columns] = split(out)


def condition_pair(prepared, straight, swapped, after):
    out = jax.ShapeDtypeStruct((4 * straight.shape[0], straight.shape[1]), jnp.bfloat16)
    return pl.pallas_call(
        condition_kernel,
        out_shape=[out, out],
        in_specs=[VMEM] * 6 + [ANYWHERE],
        out_specs=[VMEM] * 2,
        cost_estimate=FREE,
        compiler_params=pltpu.CompilerParams(vmem_limit_bytes=24 << 20),
    )(*prepared, straight, swapped, after)


def block_scores_of(high, low, t_ref):
    return split_scores_of(high, low, *split(t_ref[...]))


def split_scores_of(high, low, t_high, t_low):
    rows = t_high.shape[0]
    dot = functools.partial(
        lax.dot_general, dimension_numbers=(((1,), (1,)), ((), ())), preferred_element_type=jnp.float32
    )
    both = dot(jnp.concatenate([t_high, t_low], axis=0), high)
    return both[rows:] + dot(t_high, low) + both[:rows]


def scores_kernel(high_ref, low_ref, t_ref, out_ref):
    out_ref[...] = block_scores_of(high_ref[...], low_ref[...], t_ref)


def score(conditioned, block):
    return pl.pallas_call(
        scores_kernel,
        out_shape=jax.ShapeDtypeStruct((block.shape[0], conditioned[0].shape[0]), jnp.float32),
        in_specs=[VMEM] * 3,
        out_specs=VMEM,
        cost_estimate=FREE,
        compiler_params=pltpu.CompilerParams(vmem_limit_bytes=16 << 20),
    )(*conditioned, block)


def last_kernel(flip_ref, high_ref, low_ref, near_ref, own_ref, far_ref, cross_ref, keep_ref, give_ref):
    near = block_scores_of(high_ref[...], low_ref[...], near_ref)
    own, far, cross = own_ref[...], far_ref[...], cross_ref[...]
    flip = flip_ref[0] != 0
    keep_ref[0], give_ref[0] = jnp.where(flip, near, own), jnp.where(flip, own, near)
    keep_ref[1], give_ref[1] = jnp.where(flip, cross, far), jnp.where(flip, far, cross)


def last_scores(conditioned, near, others, flip):
    out = jax.ShapeDtypeStruct((2, *others[0].shape), jnp.float32)
    return pl.pallas_call(
        last_kernel,
        out_shape=[out, out],
        in_specs=[pl.BlockSpec(memory_space=pltpu.SMEM)] + [VMEM] * 6,
        out_specs=[VMEM] * 2,
        cost_estimate=FREE,
        compiler_params=pltpu.CompilerParams(vmem_limit_bytes=16 << 20),
    )(flip.reshape(1), *conditioned, near, *others)


def split_kernel(given_ref, high_ref, low_ref):
    high_ref[...], low_ref[...] = split(given_ref[...])


def split_block(block):
    out = jax.ShapeDtypeStruct(block.shape, jnp.bfloat16)
    return pl.pallas_call(
        split_kernel,
        out_shape=[out, out],
        in_specs=[VMEM],
        out_specs=[VMEM] * 2,
        cost_estimate=SPLIT_COST,
        compiler_params=pltpu.CompilerParams(vmem_limit_bytes=16 << 20),
    )(block)


def split_scores_kernel(high_ref, low_ref, t_high_ref, t_low_ref, out_ref):
    out_ref[...] = split_scores_of(high_ref[...], low_ref[...], t_high_ref[...], t_low_ref[...])


def split_score(conditioned, halves):
    return pl.pallas_call(
        split_scores_kernel,
        out_shape=jax.ShapeDtypeStruct((halves[0].shape[0], conditioned[0].shape[0]), jnp.float32),
        in_specs=[VMEM] * 4,
        out_specs=VMEM,
        cost_estimate=FREE,
        compiler_params=pltpu.CompilerParams(vmem_limit_bytes=16 << 20),
    )(*conditioned, *halves)


def swap_both(array, row_bit, feat_bit):
    nrow, nfeat = lax.axis_size("row"), lax.axis_size("feat")
    pairs = [
        (r * nfeat + f, (r ^ row_bit) * nfeat + (f ^ feat_bit)) for r in range(nrow) for f in range(nfeat)
    ]
    return lax.ppermute(array, ("row", "feat"), pairs)


def four_shards(queries, train_rows, inv_gram):
    qrows = queries.shape[0]
    row, feat = lax.axis_index("row"), lax.axis_index("feat")
    q_others, t_others, t_mine = pack(queries, train_rows)
    q_pair = swap(q_others, "row", 1)
    cross = swap(t_others, "row", 3)
    far = swap(t_mine, "row", 2)
    near = swap(t_others, "row", 1)
    halves = split_block(cross)
    conditioned = condition_pair(prepare(queries, inv_gram), q_pair, swap(q_pair, "grp", 1), halves[1])

    others = [score(conditioned, t_mine), score(conditioned, far), split_score(conditioned, halves)]
    flip = (row ^ feat) % 2
    keep, give = last_scores(conditioned, near, others, flip)
    keep = keep + swap(give, "feat", 1)
    odd = ((row ^ feat) // 2) % 2 == 1
    give, keep = jnp.where(odd, keep[0], keep[1]), jnp.where(odd, keep[1], keep[0])
    own, other = slice(0, qrows), slice(qrows, 2 * qrows)
    there = swap_both(keep[:, other], 1, 0)
    across = swap_both(give[:, other], 1, 2)
    beside = swap_both(give[:, own], 0, 2)
    return (keep[:, own] + there + across + beside).T


def solution(mesh):
    four = mesh.shape["row"] == 4 and mesh.shape["feat"] == 4
    return jax.shard_map(
        four_shards if four else any_shards,
        mesh=mesh,
        in_specs=(P("row", "feat"), P(("grp", "row"), "feat"), P("feat", None, None)),
        out_specs=P("row", ("grp", "feat")),
        check_vma=False,
    )
```

```python
import functools

import jax
import jax.numpy as jnp
from jax import lax
from jax.experimental import pallas as pl
from jax.experimental.pallas import tpu as pltpu
from jax.sharding import PartitionSpec as P

HIGHEST = lax.Precision.HIGHEST
ANYWHERE = pl.BlockSpec(memory_space=pl.ANY)
VMEM = pl.BlockSpec(memory_space=pltpu.VMEM)
TURNS = ((3, 2, 1, 0), (2, 0, 3, 1), (1, 3, 0, 2))
FREE = pl.CostEstimate(flops=0, bytes_accessed=0, transcendentals=0)


def send(array, axis, to):
    devices = lax.axis_size(axis)
    return lax.ppermute(array, axis, [(i, to(i)) for i in range(devices)])


def swap(array, axis, bit):
    return send(array, axis, lambda i: i ^ bit)


SPLIT_COST = pl.CostEstimate(flops=8589934592, bytes_accessed=67108864, transcendentals=0)
PREPARE_COST = pl.CostEstimate(flops=1 << 31, bytes_accessed=8 << 20, transcendentals=0)


def condition(queries, inv_gram):
    rows = queries.shape[0]
    nblocks, modsize = inv_gram.shape[0], inv_gram.shape[1]
    blocks = queries.reshape(rows, nblocks, modsize)
    out = jnp.einsum("qbi,bij->qbj", blocks, inv_gram, precision=HIGHEST)
    return out.reshape(rows, nblocks * modsize)


def block_scores(left, right):
    return jnp.dot(left, right.T, precision=HIGHEST, preferred_element_type=jnp.float32)


def any_shards(queries, train_rows, inv_gram):
    qrows, fshard = queries.shape
    trows = train_rows.shape[0]
    nrow, nfeat = lax.axis_size("row"), lax.axis_size("feat")
    row, feat = lax.axis_index("row"), lax.axis_index("feat")
    half, nmod = fshard // 2, inv_gram.shape[0] // 2
    side = row % 2

    def mine(array):
        return lax.dynamic_slice_in_dim(array, side * half, half, 1)

    def others(array):
        return lax.dynamic_slice_in_dim(array, (1 - side) * half, half, 1)

    q_mine, q_others = mine(queries), others(queries)
    t_mine, t_others = mine(train_rows), others(train_rows)
    q_pair = swap(q_others, "row", 1)
    blocks = [(t_mine, row), (swap(t_others, "row", 1), row ^ 1)]
    for step in range(2, nrow, 2):
        blocks.append((send(t_mine, "row", lambda i: (i + step) % nrow), (row - step) % nrow))
        blocks.append((send(t_others, "row", lambda i: ((i + step) % nrow) ^ 1), ((row ^ 1) - step) % nrow))

    gram = lax.dynamic_slice_in_dim(inv_gram, side * nmod, nmod, 0)
    conditioned = condition(jnp.concatenate([q_mine, q_pair], axis=0), gram)
    partial = jnp.zeros((nrow, 2 * qrows, trows), jnp.float32)
    for block, source in blocks:
        partial = lax.dynamic_update_slice(partial, block_scores(conditioned, block)[None], (source, 0, 0))

    left, bit = nfeat, 1
    partial = partial.reshape(nfeat, nrow // nfeat, 2 * qrows, trows)
    while left > 1:
        pairs = partial.reshape(left // 2, 2, *partial.shape[1:])
        odd = (feat // bit) % 2 == 1
        keep = jnp.where(odd, pairs[:, 1], pairs[:, 0])
        give = jnp.where(odd, pairs[:, 0], pairs[:, 1])
        partial = keep + swap(give, "feat", bit)
        left, bit = left // 2, bit * 2
    partial = partial[0]
    scores = partial[:, :qrows] + swap(partial[:, qrows:], "row", 1)
    return scores.transpose(1, 0, 2).reshape(qrows, -1)


def at_row(table):
    row = lax.axis_index("row")
    return sum(jnp.where(row == i, value, 0) for i, value in enumerate(table))


def pack_kernel(*refs, turns, queries):
    outs, sems = refs[-1 - len(turns) - queries : -1], refs[-1]
    t_ref = refs[0]
    half = t_ref.shape[1] // 2

    def columns(which):
        return pl.ds(pl.multiple_of(which * half, half), half)

    copies = [
        (t_ref.at[:, columns(at_row([target % 2 for target in TURNS[turn]]))], out) for turn, out in zip(turns, outs)
    ]
    if queries:
        qrows = outs[-1].shape[0]
        rows = pl.ds(pl.multiple_of(lax.axis_index("grp") * qrows, qrows), qrows)
        copies.append((refs[1].at[rows, columns(1 - lax.axis_index("row") % 2)], outs[-1]))
    copies = [pltpu.make_async_copy(*pair, sems.at[i]) for i, pair in enumerate(copies)]
    for copy in copies:
        copy.start()
    for copy in copies:
        copy.wait()


def pack(turns, train_rows, *rest):
    trows, half = train_rows.shape[0], train_rows.shape[1] // 2
    rows = [trows for _ in turns] + [array.shape[0] // 2 for array in rest[:1]]
    return pl.pallas_call(
        functools.partial(pack_kernel, turns=turns, queries=len(rest[:1])),
        out_shape=[pltpu.VMEM((size, half), jnp.float32) for size in rows],
        in_specs=[ANYWHERE] * (1 + len(rest)),
        out_specs=[VMEM] * len(rows),
        scratch_shapes=[pltpu.SemaphoreType.DMA((len(rows),))],
        cost_estimate=FREE,
    )(train_rows, *rest)


def split(x):
    high = x.astype(jnp.bfloat16)
    return high, (x - high.astype(jnp.float32)).astype(jnp.bfloat16)


def dot3(left, right, dimension_numbers):
    dot = functools.partial(
        lax.dot_general, dimension_numbers=dimension_numbers, preferred_element_type=jnp.float32
    )
    return dot(left[0], right[1]) + dot(left[1], right[0]) + dot(left[0], right[0])


PLAIN = (((1,), (0,)), ((), ()))


def prepare_kernel(q_hbm, gram_hbm, t_hbm, high_ref, low_ref, g_high_ref, g_low_ref, t_ref, q_ref, gram_ref, sems):
    side = lax.axis_index("row") % 2
    nmod, modsize = gram_ref.shape[0], gram_ref.shape[1]
    half = nmod * modsize
    columns = pl.ds(pl.multiple_of(side * half, half), half)
    get_q = pltpu.make_async_copy(q_hbm.at[:, columns], q_ref, sems.at[0])
    get_t = pltpu.make_async_copy(t_hbm.at[:, columns], t_ref, sems.at[2])
    get_gram = pltpu.make_async_copy(gram_hbm.at[pl.ds(side * nmod, nmod)], gram_ref, sems.at[1])
    for copy in (get_q, get_gram, get_t):
        copy.start()
    for copy in (get_q, get_gram, get_t):
        copy.wait()
    for m in range(nmod):
        columns = slice(m * modsize, (m + 1) * modsize)
        gram = split(gram_ref[m])
        g_high_ref[m], g_low_ref[m] = gram
        high_ref[:, columns], low_ref[:, columns] = split(dot3(split(q_ref[:, columns]), gram, PLAIN))


def prepare(queries, inv_gram, train_rows):
    qrows, half = queries.shape[0], queries.shape[1] // 2
    nmod, modsize = inv_gram.shape[0] // 2, inv_gram.shape[1]
    conditioned = pltpu.VMEM((qrows, half), jnp.bfloat16)
    gram = pltpu.VMEM((nmod, modsize, modsize), jnp.bfloat16)
    return pl.pallas_call(
        prepare_kernel,
        out_shape=[conditioned, conditioned, gram, gram, pltpu.VMEM((train_rows.shape[0], half), jnp.float32)],
        in_specs=[ANYWHERE] * 3,
        out_specs=[VMEM] * 5,
        scratch_shapes=[
            pltpu.VMEM((qrows, half), jnp.float32),
            pltpu.VMEM((nmod, modsize, modsize), jnp.float32),
            pltpu.SemaphoreType.DMA((3,)),
        ],
        cost_estimate=PREPARE_COST,
        compiler_params=pltpu.CompilerParams(vmem_limit_bytes=24 << 20),
    )(queries, inv_gram, train_rows)


def condition_kernel(own_high, own_low, g_high, g_low, straight_ref, swapped_ref, after_ref, high_ref, low_ref):
    qrows, modsize = own_high.shape[0], g_high.shape[1]
    first = lax.axis_index("grp") == 0
    high_ref[:qrows], low_ref[:qrows] = own_high[...], own_low[...]
    for m in range(g_high.shape[0]):
        columns = slice(m * modsize, (m + 1) * modsize)
        straight, swapped = straight_ref[:, columns], swapped_ref[:, columns]
        pair = [jnp.where(first, straight, swapped), jnp.where(first, swapped, straight)]
        out = dot3(split(jnp.concatenate(pair, axis=0)), (g_high[m], g_low[m]), PLAIN)
        high_ref[qrows:, columns], low_ref[qrows:, columns] = split(out)


def condition_pair(prepared, straight, swapped, after):
    out = jax.ShapeDtypeStruct((4 * straight.shape[0], straight.shape[1]), jnp.bfloat16)
    return pl.pallas_call(
        condition_kernel,
        out_shape=[out, out],
        in_specs=[VMEM] * 6 + [ANYWHERE],
        out_specs=[VMEM] * 2,
        cost_estimate=FREE,
        compiler_params=pltpu.CompilerParams(vmem_limit_bytes=24 << 20),
    )(*prepared, straight, swapped, after)


def block_scores_of(high, low, t_ref):
    return split_scores_of(high, low, *split(t_ref[...]))


def split_scores_of(high, low, t_high, t_low):
    rows = t_high.shape[0]
    dot = functools.partial(
        lax.dot_general, dimension_numbers=(((1,), (1,)), ((), ())), preferred_element_type=jnp.float32
    )
    both = dot(jnp.concatenate([t_high, t_low], axis=0), high)
    return both[rows:] + dot(t_high, low) + both[:rows]


def scores_kernel(high_ref, low_ref, t_ref, out_ref):
    out_ref[...] = block_scores_of(high_ref[...], low_ref[...], t_ref)


def score(conditioned, block):
    return pl.pallas_call(
        scores_kernel,
        out_shape=jax.ShapeDtypeStruct((block.shape[0], conditioned[0].shape[0]), jnp.float32),
        in_specs=[VMEM] * 3,
        out_specs=VMEM,
        cost_estimate=FREE,
        compiler_params=pltpu.CompilerParams(vmem_limit_bytes=16 << 20),
    )(*conditioned, block)


def last_kernel(high_ref, low_ref, t_ref, own_ref, first_ref, second_ref, keep_ref, give_ref):
    third = block_scores_of(high_ref[...], low_ref[...], t_ref)
    own, first, second = own_ref[...], first_ref[...], second_ref[...]
    kinds = [at_row([row ^ targets.index(row) for row in range(len(targets))]) for targets in TURNS]

    def of_kind(kind):
        return jnp.where(kinds[0] == kind, first, jnp.where(kinds[1] == kind, second, third))

    near, far, cross = of_kind(1), of_kind(2), of_kind(3)
    flip = (lax.axis_index("row") + lax.axis_index("feat")) % 2 != 0
    keep_ref[0], give_ref[0] = jnp.where(flip, near, own), jnp.where(flip, own, near)
    keep_ref[1], give_ref[1] = jnp.where(flip, cross, far), jnp.where(flip, far, cross)


def last_scores(conditioned, third, others):
    out = jax.ShapeDtypeStruct((2, *others[0].shape), jnp.float32)
    return pl.pallas_call(
        last_kernel,
        out_shape=[out, out],
        in_specs=[VMEM] * 6,
        out_specs=[VMEM] * 2,
        cost_estimate=FREE,
        compiler_params=pltpu.CompilerParams(vmem_limit_bytes=16 << 20),
    )(*conditioned, third, *others)


def split_kernel(given_ref, high_ref, low_ref):
    high_ref[...], low_ref[...] = split(given_ref[...])


def split_block(block):
    out = jax.ShapeDtypeStruct(block.shape, jnp.bfloat16)
    return pl.pallas_call(
        split_kernel,
        out_shape=[out, out],
        in_specs=[VMEM],
        out_specs=[VMEM] * 2,
        cost_estimate=SPLIT_COST,
        compiler_params=pltpu.CompilerParams(vmem_limit_bytes=16 << 20),
    )(block)


def split_scores_kernel(high_ref, low_ref, t_high_ref, t_low_ref, out_ref):
    out_ref[...] = split_scores_of(high_ref[...], low_ref[...], t_high_ref[...], t_low_ref[...])


def split_score(conditioned, halves):
    return pl.pallas_call(
        split_scores_kernel,
        out_shape=jax.ShapeDtypeStruct((halves[0].shape[0], conditioned[0].shape[0]), jnp.float32),
        in_specs=[VMEM] * 4,
        out_specs=VMEM,
        cost_estimate=FREE,
        compiler_params=pltpu.CompilerParams(vmem_limit_bytes=16 << 20),
    )(*conditioned, *halves)


def swap_both(array, row_bit, feat_bit):
    nrow, nfeat = lax.axis_size("row"), lax.axis_size("feat")
    pairs = [
        (r * nfeat + f, (r ^ row_bit) * nfeat + (f ^ feat_bit)) for r in range(nrow) for f in range(nfeat)
    ]
    return lax.ppermute(array, ("row", "feat"), pairs)


def four_shards(queries, train_rows, inv_gram):
    qrows = queries.shape[0]
    row, feat = lax.axis_index("row"), lax.axis_index("feat")
    (t_first,) = pack((0,), train_rows)
    *t_later, q_others = pack((1, 2), train_rows, queries, t_first)
    q_pair = swap(q_others, "row", 1)
    first, second, third = [
        send(block, "row", lambda i: targets[i]) for block, targets in zip([t_first, *t_later], TURNS)
    ]
    halves = split_block(first)
    *prepared, t_mine = prepare(queries, inv_gram, train_rows)
    conditioned = condition_pair(prepared, q_pair, swap(q_pair, "grp", 1), halves[1])

    others = [score(conditioned, t_mine), split_score(conditioned, halves), score(conditioned, second)]
    keep, give = last_scores(conditioned, third, others)
    keep = keep + swap(give, "feat", 1)
    odd = ((row ^ feat) // 2) % 2 == 1
    give, keep = jnp.where(odd, keep[0], keep[1]), jnp.where(odd, keep[1], keep[0])
    own, other = slice(0, qrows), slice(qrows, 2 * qrows)
    there = swap_both(keep[:, other], 1, 0)
    across = swap_both(give[:, other], 1, 2)
    beside = swap_both(give[:, own], 0, 2)
    return (keep[:, own] + there + across + beside).T


def solution(mesh):
    four = mesh.shape["row"] == 4 and mesh.shape["feat"] == 4
    return jax.shard_map(
        four_shards if four else any_shards,
        mesh=mesh,
        in_specs=(P("row", "feat"), P(("grp", "row"), "feat"), P("feat", None, None)),
        out_specs=P("row", ("grp", "feat")),
        check_vma=False,
    )
```

```python
import functools

import jax
import jax.numpy as jnp
from jax import lax
from jax.experimental import pallas as pl
from jax.experimental.pallas import tpu as pltpu
from jax.sharding import PartitionSpec as P

HIGHEST = lax.Precision.HIGHEST
ANYWHERE = pl.BlockSpec(memory_space=pl.ANY)
VMEM = pl.BlockSpec(memory_space=pltpu.VMEM)
TURNS = ((3, 2, 1, 0), (2, 0, 3, 1), (1, 3, 0, 2))
FREE = pl.CostEstimate(flops=0, bytes_accessed=0, transcendentals=0)


def send(array, axis, to):
    devices = lax.axis_size(axis)
    return lax.ppermute(array, axis, [(i, to(i)) for i in range(devices)])


def swap(array, axis, bit):
    return send(array, axis, lambda i: i ^ bit)


MID_COST = pl.CostEstimate(flops=1 << 31, bytes_accessed=8 << 20, transcendentals=0)
SPLIT_COST = pl.CostEstimate(flops=8589934592, bytes_accessed=67108864, transcendentals=0)
PREPARE_COST = pl.CostEstimate(flops=1 << 31, bytes_accessed=8 << 20, transcendentals=0)


def condition(queries, inv_gram):
    rows = queries.shape[0]
    nblocks, modsize = inv_gram.shape[0], inv_gram.shape[1]
    blocks = queries.reshape(rows, nblocks, modsize)
    out = jnp.einsum("qbi,bij->qbj", blocks, inv_gram, precision=HIGHEST)
    return out.reshape(rows, nblocks * modsize)


def block_scores(left, right):
    return jnp.dot(left, right.T, precision=HIGHEST, preferred_element_type=jnp.float32)


def any_shards(queries, train_rows, inv_gram):
    qrows, fshard = queries.shape
    trows = train_rows.shape[0]
    nrow, nfeat = lax.axis_size("row"), lax.axis_size("feat")
    row, feat = lax.axis_index("row"), lax.axis_index("feat")
    half, nmod = fshard // 2, inv_gram.shape[0] // 2
    side = row % 2

    def mine(array):
        return lax.dynamic_slice_in_dim(array, side * half, half, 1)

    def others(array):
        return lax.dynamic_slice_in_dim(array, (1 - side) * half, half, 1)

    q_mine, q_others = mine(queries), others(queries)
    t_mine, t_others = mine(train_rows), others(train_rows)
    q_pair = swap(q_others, "row", 1)
    blocks = [(t_mine, row), (swap(t_others, "row", 1), row ^ 1)]
    for step in range(2, nrow, 2):
        blocks.append((send(t_mine, "row", lambda i: (i + step) % nrow), (row - step) % nrow))
        blocks.append((send(t_others, "row", lambda i: ((i + step) % nrow) ^ 1), ((row ^ 1) - step) % nrow))

    gram = lax.dynamic_slice_in_dim(inv_gram, side * nmod, nmod, 0)
    conditioned = condition(jnp.concatenate([q_mine, q_pair], axis=0), gram)
    partial = jnp.zeros((nrow, 2 * qrows, trows), jnp.float32)
    for block, source in blocks:
        partial = lax.dynamic_update_slice(partial, block_scores(conditioned, block)[None], (source, 0, 0))

    left, bit = nfeat, 1
    partial = partial.reshape(nfeat, nrow // nfeat, 2 * qrows, trows)
    while left > 1:
        pairs = partial.reshape(left // 2, 2, *partial.shape[1:])
        odd = (feat // bit) % 2 == 1
        keep = jnp.where(odd, pairs[:, 1], pairs[:, 0])
        give = jnp.where(odd, pairs[:, 0], pairs[:, 1])
        partial = keep + swap(give, "feat", bit)
        left, bit = left // 2, bit * 2
    partial = partial[0]
    scores = partial[:, :qrows] + swap(partial[:, qrows:], "row", 1)
    return scores.transpose(1, 0, 2).reshape(qrows, -1)


def at_row(table):
    row = lax.axis_index("row")
    return sum(jnp.where(row == i, value, 0) for i, value in enumerate(table))


def pack_kernel(*refs, turns, queries):
    outs, sems = refs[-1 - len(turns) - queries : -1], refs[-1]
    t_ref = refs[0]
    half = t_ref.shape[1] // 2

    def columns(which):
        return pl.ds(pl.multiple_of(which * half, half), half)

    other = (lax.axis_index("row") + lax.axis_index("feat")) % 2 != 0
    wanted = [at_row([target % 2 for target in targets]) for targets in TURNS]
    wanted = [wanted[0], jnp.where(other, wanted[2], wanted[1]), jnp.where(other, wanted[1], wanted[2])]
    copies = [(t_ref.at[:, columns(wanted[turn])], out) for turn, out in zip(turns, outs)]
    if queries:
        qrows = outs[-1].shape[0]
        rows = pl.ds(pl.multiple_of(lax.axis_index("grp") * qrows, qrows), qrows)
        copies.append((refs[1].at[rows, columns(1 - lax.axis_index("row") % 2)], outs[-1]))
    copies = [pltpu.make_async_copy(*pair, sems.at[i]) for i, pair in enumerate(copies)]
    for copy in copies:
        copy.start()
    for copy in copies:
        copy.wait()


def pack(turns, train_rows, *rest):
    trows, half = train_rows.shape[0], train_rows.shape[1] // 2
    rows = [trows for _ in turns] + [array.shape[0] // 2 for array in rest[:1]]
    return pl.pallas_call(
        functools.partial(pack_kernel, turns=turns, queries=len(rest[:1])),
        out_shape=[pltpu.VMEM((size, half), jnp.float32) for size in rows],
        in_specs=[ANYWHERE] * (1 + len(rest)),
        out_specs=[VMEM] * len(rows),
        scratch_shapes=[pltpu.SemaphoreType.DMA((len(rows),))],
        cost_estimate=FREE,
    )(train_rows, *rest)


def split(x):
    high = x.astype(jnp.bfloat16)
    return high, (x - high.astype(jnp.float32)).astype(jnp.bfloat16)


def dot3(left, right, dimension_numbers):
    dot = functools.partial(
        lax.dot_general, dimension_numbers=dimension_numbers, preferred_element_type=jnp.float32
    )
    return dot(left[0], right[1]) + dot(left[1], right[0]) + dot(left[0], right[0])


PLAIN = (((1,), (0,)), ((), ()))


def prepare_kernel(q_hbm, gram_hbm, t_hbm, high_ref, low_ref, g_high_ref, g_low_ref, t_ref, q_ref, gram_ref, sems):
    side = lax.axis_index("row") % 2
    nmod, modsize = gram_ref.shape[0], gram_ref.shape[1]
    half = nmod * modsize
    columns = pl.ds(pl.multiple_of(side * half, half), half)
    get_q = pltpu.make_async_copy(q_hbm.at[:, columns], q_ref, sems.at[0])
    get_t = pltpu.make_async_copy(t_hbm.at[:, columns], t_ref, sems.at[2])
    get_gram = pltpu.make_async_copy(gram_hbm.at[pl.ds(side * nmod, nmod)], gram_ref, sems.at[1])
    for copy in (get_q, get_gram, get_t):
        copy.start()
    for copy in (get_q, get_gram, get_t):
        copy.wait()
    for m in range(nmod):
        columns = slice(m * modsize, (m + 1) * modsize)
        gram = split(gram_ref[m])
        g_high_ref[m], g_low_ref[m] = gram
        high_ref[:, columns], low_ref[:, columns] = split(dot3(split(q_ref[:, columns]), gram, PLAIN))


def prepare(queries, inv_gram, train_rows):
    qrows, half = queries.shape[0], queries.shape[1] // 2
    nmod, modsize = inv_gram.shape[0] // 2, inv_gram.shape[1]
    conditioned = pltpu.VMEM((qrows, half), jnp.bfloat16)
    gram = pltpu.VMEM((nmod, modsize, modsize), jnp.bfloat16)
    return pl.pallas_call(
        prepare_kernel,
        out_shape=[conditioned, conditioned, gram, gram, pltpu.VMEM((train_rows.shape[0], half), jnp.float32)],
        in_specs=[ANYWHERE] * 3,
        out_specs=[VMEM] * 5,
        scratch_shapes=[
            pltpu.VMEM((qrows, half), jnp.float32),
            pltpu.VMEM((nmod, modsize, modsize), jnp.float32),
            pltpu.SemaphoreType.DMA((3,)),
        ],
        cost_estimate=PREPARE_COST,
        compiler_params=pltpu.CompilerParams(vmem_limit_bytes=24 << 20),
    )(queries, inv_gram, train_rows)


def condition_kernel(own_high, own_low, g_high, g_low, straight_ref, swapped_ref, after_ref, high_ref, low_ref, whole_ref):
    qrows, modsize = own_high.shape[0], g_high.shape[1]
    first = lax.axis_index("grp") == 0
    high_ref[:qrows], low_ref[:qrows] = own_high[...], own_low[...]
    for m in range(g_high.shape[0]):
        columns = slice(m * modsize, (m + 1) * modsize)
        straight, swapped = straight_ref[:, columns], swapped_ref[:, columns]
        pair = [jnp.where(first, straight, swapped), jnp.where(first, swapped, straight)]
        out = dot3(split(jnp.concatenate(pair, axis=0)), (g_high[m], g_low[m]), PLAIN)
        high_ref[qrows:, columns], low_ref[qrows:, columns] = split(out)
    whole_ref[...] = high_ref[...].astype(jnp.float32) + low_ref[...].astype(jnp.float32)


def condition_pair(prepared, straight, swapped, after):
    out = jax.ShapeDtypeStruct((4 * straight.shape[0], straight.shape[1]), jnp.bfloat16)
    return pl.pallas_call(
        condition_kernel,
        out_shape=[out, out, jax.ShapeDtypeStruct(out.shape, jnp.float32)],
        in_specs=[VMEM] * 6 + [ANYWHERE],
        out_specs=[VMEM] * 3,
        cost_estimate=FREE,
        compiler_params=pltpu.CompilerParams(vmem_limit_bytes=24 << 20),
    )(*prepared, straight, swapped, after)


def split_rows(block):
    rows = block.shape[0]
    if rows % 16:
        block = jnp.concatenate([block, jnp.zeros((-rows % 16, block.shape[1]), block.dtype)], axis=0)
    return split(block)


def split_scores_of(high, low, t_high, t_low):
    rows = t_high.shape[0]
    dot = functools.partial(
        lax.dot_general, dimension_numbers=(((1,), (1,)), ((), ())), preferred_element_type=jnp.float32
    )
    both = dot(jnp.concatenate([t_high, t_low], axis=0), high)
    return both[rows:] + dot(t_high, low) + both[:rows]


def scores_kernel(high_ref, low_ref, t_ref, out_ref):
    out_ref[...] = split_scores_of(high_ref[...], low_ref[...], *split_rows(t_ref[...]))[: out_ref.shape[0]]


def score(conditioned, block):
    return pl.pallas_call(
        scores_kernel,
        out_shape=jax.ShapeDtypeStruct((block.shape[0], conditioned[0].shape[0]), jnp.float32),
        in_specs=[VMEM] * 3,
        out_specs=VMEM,
        cost_estimate=FREE,
        compiler_params=pltpu.CompilerParams(vmem_limit_bytes=16 << 20),
    )(*conditioned, block)


def last_kernel(*refs):
    mine, other, second, third = refs[:2], refs[2:4], refs[4:6], refs[6:8]
    early_ref, late_ref = refs[8], refs[13]
    row, feat = lax.axis_index("row"), lax.axis_index("feat")
    here = feat % 2 == row // 2

    def scores(left, right):
        left, right = [ref[...] for ref in left], [ref[...] for ref in right]
        total = split_scores_of(*left, *[ref[...] for ref in third])
        return (total + split_scores_of(*right, *[ref[...] for ref in second]))[: late_ref.shape[0]]

    @pl.when(here)
    def _():
        late_ref[...] = scores(mine, other)

    @pl.when(jnp.logical_not(here))
    def _():
        late_ref[...] = scores(other, mine)

    late, early = late_ref[...], early_ref[...]
    own = (row + feat + row // 2 + feat // 2) % 2 != 0
    qrows = early.shape[1] // 2
    keep, give = jnp.where(own, late, early), jnp.where(own, early, late)
    refs[9][...], refs[10][...] = keep[:, :qrows], keep[:, qrows:]
    refs[11][...], refs[12][...] = give[:, :qrows], give[:, qrows:]


def last_scores(mine, other, second, third, early):
    trows, queries = early.shape
    out = jax.ShapeDtypeStruct((trows, queries // 2), jnp.float32)
    return pl.pallas_call(
        last_kernel,
        out_shape=[out] * 4,
        in_specs=[VMEM] * 9,
        out_specs=[VMEM] * 4,
        scratch_shapes=[pltpu.VMEM((trows, queries), jnp.float32)],
        cost_estimate=FREE,
        compiler_params=pltpu.CompilerParams(vmem_limit_bytes=16 << 20),
    )(*mine, *other, *second, *third, early)


def split_kernel(given_ref, high_ref, low_ref):
    high_ref[...], low_ref[...] = split_rows(given_ref[...])


def split_block(block, cost):
    rows, columns = block.shape
    out = jax.ShapeDtypeStruct((rows + -rows % 16, columns), jnp.bfloat16)
    return pl.pallas_call(
        split_kernel,
        out_shape=[out, out],
        in_specs=[VMEM],
        out_specs=[VMEM] * 2,
        cost_estimate=cost,
        compiler_params=pltpu.CompilerParams(vmem_limit_bytes=16 << 20),
    )(block)


def split_scores_kernel(high_ref, low_ref, t_high_ref, t_low_ref, out_ref):
    out = split_scores_of(high_ref[...], low_ref[...], t_high_ref[...], t_low_ref[...])
    out_ref[...] = out[: out_ref.shape[0]]


def split_score(conditioned, halves, trows):
    return pl.pallas_call(
        split_scores_kernel,
        out_shape=jax.ShapeDtypeStruct((trows, conditioned[0].shape[0]), jnp.float32),
        in_specs=[VMEM] * 4,
        out_specs=VMEM,
        cost_estimate=FREE,
        compiler_params=pltpu.CompilerParams(vmem_limit_bytes=16 << 20),
    )(*conditioned, *halves)


def permute(array, to):
    nrow, nfeat = lax.axis_size("row"), lax.axis_size("feat")
    pairs = []
    for row in range(nrow):
        for feat in range(nfeat):
            to_row, to_feat = to(row, feat)
            pairs.append((row * nfeat + feat, to_row * nfeat + to_feat))
    return lax.ppermute(array, ("row", "feat"), pairs)


def mixed(array, turn):
    def to(row, feat):
        straight = (row + feat) % 2 == 0
        return TURNS[turn if straight else 3 - turn][row], feat if straight else feat ^ 1

    return permute(array, to)


def four_shards(queries, train_rows, inv_gram):
    row, feat = lax.axis_index("row"), lax.axis_index("feat")
    (t_first,) = pack((0,), train_rows)
    t_second, t_third, q_others = pack((1, 2), train_rows, queries, t_first)
    q_pair = swap(q_others, "row", 1)
    cross = send(t_first, "row", lambda i: TURNS[0][i])
    second, third = mixed(t_second, 1), mixed(t_third, 2)
    halves = split_block(cross, SPLIT_COST)
    *prepared, t_mine = prepare(queries, inv_gram, train_rows)
    *conditioned, whole = condition_pair(prepared, q_pair, swap(q_pair, "grp", 1), halves[1])
    other = split_block(swap(whole, "feat", 1), FREE)

    own_core = (row + feat) % 2 == 0
    own, cross = score(conditioned, t_mine), split_score(conditioned, halves, t_mine.shape[0])
    early = jnp.where(own_core, own, cross) + swap(jnp.where(own_core, cross, own), "feat", 1)
    second, third = split_block(second, FREE), split_block(third, SPLIT_COST)
    keep, keep_pair, give, give_pair = last_scores(conditioned, other, second, third, early)
    there = permute(keep_pair, lambda r, f: (r ^ 1, f))
    across = permute(give_pair, lambda r, f: (r ^ 1, f ^ 2))
    beside = permute(give, lambda r, f: (r, f ^ 2))
    return (keep + there + across + beside).T


def solution(mesh):
    four = mesh.shape["row"] == 4 and mesh.shape["feat"] == 4
    return jax.shard_map(
        four_shards if four else any_shards,
        mesh=mesh,
        in_specs=(P("row", "feat"), P(("grp", "row"), "feat"), P("feat", None, None)),
        out_specs=P("row", ("grp", "feat")),
        check_vma=False,
    )
```

```python
import functools

import jax
import jax.numpy as jnp
from jax import lax
from jax.experimental import pallas as pl
from jax.experimental.pallas import tpu as pltpu
from jax.sharding import PartitionSpec as P

HIGHEST = lax.Precision.HIGHEST
ANYWHERE = pl.BlockSpec(memory_space=pl.ANY)
VMEM = pl.BlockSpec(memory_space=pltpu.VMEM)
TURNS = ((3, 2, 1, 0), (2, 0, 3, 1), (1, 3, 0, 2))
FREE = pl.CostEstimate(flops=0, bytes_accessed=0, transcendentals=0)


def send(array, axis, to):
    devices = lax.axis_size(axis)
    return lax.ppermute(array, axis, [(i, to(i)) for i in range(devices)])


def swap(array, axis, bit):
    return send(array, axis, lambda i: i ^ bit)


MID_COST = pl.CostEstimate(flops=1 << 31, bytes_accessed=8 << 20, transcendentals=0)
SPLIT_COST = pl.CostEstimate(flops=8589934592, bytes_accessed=67108864, transcendentals=0)
PREPARE_COST = pl.CostEstimate(flops=1 << 31, bytes_accessed=8 << 20, transcendentals=0)


def condition(queries, inv_gram):
    rows = queries.shape[0]
    nblocks, modsize = inv_gram.shape[0], inv_gram.shape[1]
    blocks = queries.reshape(rows, nblocks, modsize)
    out = jnp.einsum("qbi,bij->qbj", blocks, inv_gram, precision=HIGHEST)
    return out.reshape(rows, nblocks * modsize)


def block_scores(left, right):
    return jnp.dot(left, right.T, precision=HIGHEST, preferred_element_type=jnp.float32)


def any_shards(queries, train_rows, inv_gram):
    qrows, fshard = queries.shape
    trows = train_rows.shape[0]
    nrow, nfeat = lax.axis_size("row"), lax.axis_size("feat")
    row, feat = lax.axis_index("row"), lax.axis_index("feat")
    half, nmod = fshard // 2, inv_gram.shape[0] // 2
    side = row % 2

    def mine(array):
        return lax.dynamic_slice_in_dim(array, side * half, half, 1)

    def others(array):
        return lax.dynamic_slice_in_dim(array, (1 - side) * half, half, 1)

    q_mine, q_others = mine(queries), others(queries)
    t_mine, t_others = mine(train_rows), others(train_rows)
    q_pair = swap(q_others, "row", 1)
    blocks = [(t_mine, row), (swap(t_others, "row", 1), row ^ 1)]
    for step in range(2, nrow, 2):
        blocks.append((send(t_mine, "row", lambda i: (i + step) % nrow), (row - step) % nrow))
        blocks.append((send(t_others, "row", lambda i: ((i + step) % nrow) ^ 1), ((row ^ 1) - step) % nrow))

    gram = lax.dynamic_slice_in_dim(inv_gram, side * nmod, nmod, 0)
    conditioned = condition(jnp.concatenate([q_mine, q_pair], axis=0), gram)
    partial = jnp.zeros((nrow, 2 * qrows, trows), jnp.float32)
    for block, source in blocks:
        partial = lax.dynamic_update_slice(partial, block_scores(conditioned, block)[None], (source, 0, 0))

    left, bit = nfeat, 1
    partial = partial.reshape(nfeat, nrow // nfeat, 2 * qrows, trows)
    while left > 1:
        pairs = partial.reshape(left // 2, 2, *partial.shape[1:])
        odd = (feat // bit) % 2 == 1
        keep = jnp.where(odd, pairs[:, 1], pairs[:, 0])
        give = jnp.where(odd, pairs[:, 0], pairs[:, 1])
        partial = keep + swap(give, "feat", bit)
        left, bit = left // 2, bit * 2
    partial = partial[0]
    scores = partial[:, :qrows] + swap(partial[:, qrows:], "row", 1)
    return scores.transpose(1, 0, 2).reshape(qrows, -1)


def at_row(table):
    row = lax.axis_index("row")
    return sum(jnp.where(row == i, value, 0) for i, value in enumerate(table))


def pack_kernel(*refs, turns, queries):
    outs, sems = refs[-1 - len(turns) - queries : -1], refs[-1]
    t_ref = refs[0]
    half = t_ref.shape[1] // 2

    def columns(which):
        return pl.ds(pl.multiple_of(which * half, half), half)

    other = (lax.axis_index("row") + lax.axis_index("feat")) % 2 != 0
    wanted = [at_row([target % 2 for target in targets]) for targets in TURNS]
    wanted = [wanted[0], jnp.where(other, wanted[2], wanted[1]), jnp.where(other, wanted[1], wanted[2])]
    copies = [(t_ref.at[:, columns(wanted[turn])], out) for turn, out in zip(turns, outs)]
    if queries:
        qrows = outs[-1].shape[0]
        rows = pl.ds(pl.multiple_of(lax.axis_index("grp") * qrows, qrows), qrows)
        copies.append((refs[1].at[rows, columns(1 - lax.axis_index("row") % 2)], outs[-1]))
    copies = [pltpu.make_async_copy(*pair, sems.at[i]) for i, pair in enumerate(copies)]
    for copy in copies:
        copy.start()
    for copy in copies:
        copy.wait()


def pack(turns, train_rows, *rest):
    trows, half = train_rows.shape[0], train_rows.shape[1] // 2
    rows = [trows for _ in turns] + [array.shape[0] // 2 for array in rest[:1]]
    return pl.pallas_call(
        functools.partial(pack_kernel, turns=turns, queries=len(rest[:1])),
        out_shape=[pltpu.VMEM((size, half), jnp.float32) for size in rows],
        in_specs=[ANYWHERE] * (1 + len(rest)),
        out_specs=[VMEM] * len(rows),
        scratch_shapes=[pltpu.SemaphoreType.DMA((len(rows),))],
        cost_estimate=FREE,
    )(train_rows, *rest)


def split(x):
    high = x.astype(jnp.bfloat16)
    return high, (x - high.astype(jnp.float32)).astype(jnp.bfloat16)


def dot3(left, right, dimension_numbers):
    dot = functools.partial(
        lax.dot_general, dimension_numbers=dimension_numbers, preferred_element_type=jnp.float32
    )
    return dot(left[0], right[1]) + dot(left[1], right[0]) + dot(left[0], right[0])


PLAIN = (((1,), (0,)), ((), ()))


def prepare_kernel(q_hbm, gram_hbm, t_hbm, high_ref, low_ref, g_high_ref, g_low_ref, t_ref, q_ref, gram_ref, sems):
    side = lax.axis_index("row") % 2
    nmod, modsize = gram_ref.shape[0], gram_ref.shape[1]
    half = nmod * modsize
    columns = pl.ds(pl.multiple_of(side * half, half), half)
    get_q = pltpu.make_async_copy(q_hbm.at[:, columns], q_ref, sems.at[0])
    get_t = pltpu.make_async_copy(t_hbm.at[:, columns], t_ref, sems.at[2])
    get_gram = pltpu.make_async_copy(gram_hbm.at[pl.ds(side * nmod, nmod)], gram_ref, sems.at[1])
    for copy in (get_q, get_gram, get_t):
        copy.start()
    for copy in (get_q, get_gram, get_t):
        copy.wait()
    for m in range(nmod):
        columns = slice(m * modsize, (m + 1) * modsize)
        gram = split(gram_ref[m])
        g_high_ref[m], g_low_ref[m] = gram
        high_ref[:, columns], low_ref[:, columns] = split(dot3(split(q_ref[:, columns]), gram, PLAIN))


def prepare(queries, inv_gram, train_rows):
    qrows, half = queries.shape[0], queries.shape[1] // 2
    nmod, modsize = inv_gram.shape[0] // 2, inv_gram.shape[1]
    conditioned = pltpu.VMEM((qrows, half), jnp.bfloat16)
    gram = pltpu.VMEM((nmod, modsize, modsize), jnp.bfloat16)
    return pl.pallas_call(
        prepare_kernel,
        out_shape=[conditioned, conditioned, gram, gram, pltpu.VMEM((train_rows.shape[0], half), jnp.float32)],
        in_specs=[ANYWHERE] * 3,
        out_specs=[VMEM] * 5,
        scratch_shapes=[
            pltpu.VMEM((qrows, half), jnp.float32),
            pltpu.VMEM((nmod, modsize, modsize), jnp.float32),
            pltpu.SemaphoreType.DMA((3,)),
        ],
        cost_estimate=PREPARE_COST,
        compiler_params=pltpu.CompilerParams(vmem_limit_bytes=24 << 20),
    )(queries, inv_gram, train_rows)


def condition_kernel(own_high, own_low, g_high, g_low, straight_ref, swapped_ref, after_ref, high_ref, low_ref, whole_ref):
    qrows, modsize = own_high.shape[0], g_high.shape[1]
    first = lax.axis_index("grp") == 0
    high_ref[:qrows], low_ref[:qrows] = own_high[...], own_low[...]
    for m in range(g_high.shape[0]):
        columns = slice(m * modsize, (m + 1) * modsize)
        straight, swapped = straight_ref[:, columns], swapped_ref[:, columns]
        pair = [jnp.where(first, straight, swapped), jnp.where(first, swapped, straight)]
        out = dot3(split(jnp.concatenate(pair, axis=0)), (g_high[m], g_low[m]), PLAIN)
        high_ref[qrows:, columns], low_ref[qrows:, columns] = split(out)
    whole_ref[...] = high_ref[...].astype(jnp.float32) + low_ref[...].astype(jnp.float32)


def condition_pair(prepared, straight, swapped, after):
    out = jax.ShapeDtypeStruct((4 * straight.shape[0], straight.shape[1]), jnp.bfloat16)
    return pl.pallas_call(
        condition_kernel,
        out_shape=[out, out, jax.ShapeDtypeStruct(out.shape, jnp.float32)],
        in_specs=[VMEM] * 6 + [ANYWHERE],
        out_specs=[VMEM] * 3,
        cost_estimate=FREE,
        compiler_params=pltpu.CompilerParams(vmem_limit_bytes=24 << 20),
    )(*prepared, straight, swapped, after)


def split_rows(block):
    rows = block.shape[0]
    if rows % 16:
        block = jnp.concatenate([block, jnp.zeros((-rows % 16, block.shape[1]), block.dtype)], axis=0)
    return split(block)


def split_scores_of(high, low, t_high, t_low):
    rows = t_high.shape[0]
    dot = functools.partial(
        lax.dot_general, dimension_numbers=(((1,), (1,)), ((), ())), preferred_element_type=jnp.float32
    )
    both = dot(jnp.concatenate([t_high, t_low], axis=0), high)
    return both[rows:] + dot(t_high, low) + both[:rows]


def scores_kernel(high_ref, low_ref, t_ref, out_ref):
    out_ref[...] = split_scores_of(high_ref[...], low_ref[...], *split_rows(t_ref[...]))[: out_ref.shape[0]]


def score(conditioned, block):
    return pl.pallas_call(
        scores_kernel,
        out_shape=jax.ShapeDtypeStruct((block.shape[0], conditioned[0].shape[0]), jnp.float32),
        in_specs=[VMEM] * 3,
        out_specs=VMEM,
        cost_estimate=FREE,
        compiler_params=pltpu.CompilerParams(vmem_limit_bytes=16 << 20),
    )(*conditioned, block)


def last_kernel(*refs):
    mine, other, second_ref, third = refs[:2], refs[2:4], refs[4], refs[5:7]
    early_ref, late_ref = refs[7], refs[12]
    row, feat = lax.axis_index("row"), lax.axis_index("feat")
    here = feat % 2 == row // 2

    def scores(left, right):
        left, right = [ref[...] for ref in left], [ref[...] for ref in right]
        total = split_scores_of(*left, *[ref[...] for ref in third])
        return (total + split_scores_of(*right, *split_rows(second_ref[...])))[: late_ref.shape[0]]

    @pl.when(here)
    def _():
        late_ref[...] = scores(mine, other)

    @pl.when(jnp.logical_not(here))
    def _():
        late_ref[...] = scores(other, mine)

    late, early = late_ref[...], early_ref[...]
    own = (row + feat + row // 2 + feat // 2) % 2 != 0
    qrows = early.shape[1] // 2
    keep, give = jnp.where(own, late, early), jnp.where(own, early, late)
    refs[8][...], refs[9][...] = keep[:, :qrows], keep[:, qrows:]
    refs[10][...], refs[11][...] = give[:, :qrows], give[:, qrows:]


def last_scores(mine, other, second, third, early):
    trows, queries = early.shape
    out = jax.ShapeDtypeStruct((trows, queries // 2), jnp.float32)
    return pl.pallas_call(
        last_kernel,
        out_shape=[out] * 4,
        in_specs=[VMEM] * 8,
        out_specs=[VMEM] * 4,
        scratch_shapes=[pltpu.VMEM((trows, queries), jnp.float32)],
        cost_estimate=FREE,
        compiler_params=pltpu.CompilerParams(vmem_limit_bytes=16 << 20),
    )(*mine, *other, second, *third, early)


def split_kernel(given_ref, high_ref, low_ref):
    high_ref[...], low_ref[...] = split_rows(given_ref[...])


def split_block(block, cost):
    rows, columns = block.shape
    out = jax.ShapeDtypeStruct((rows + -rows % 16, columns), jnp.bfloat16)
    return pl.pallas_call(
        split_kernel,
        out_shape=[out, out],
        in_specs=[VMEM],
        out_specs=[VMEM] * 2,
        cost_estimate=cost,
        compiler_params=pltpu.CompilerParams(vmem_limit_bytes=16 << 20),
    )(block)


def split_scores_kernel(high_ref, low_ref, t_high_ref, t_low_ref, out_ref):
    out = split_scores_of(high_ref[...], low_ref[...], t_high_ref[...], t_low_ref[...])
    out_ref[...] = out[: out_ref.shape[0]]


def split_score(conditioned, halves, trows):
    return pl.pallas_call(
        split_scores_kernel,
        out_shape=jax.ShapeDtypeStruct((trows, conditioned[0].shape[0]), jnp.float32),
        in_specs=[VMEM] * 4,
        out_specs=VMEM,
        cost_estimate=FREE,
        compiler_params=pltpu.CompilerParams(vmem_limit_bytes=16 << 20),
    )(*conditioned, *halves)


def permute(array, to):
    nrow, nfeat = lax.axis_size("row"), lax.axis_size("feat")
    pairs = []
    for row in range(nrow):
        for feat in range(nfeat):
            to_row, to_feat = to(row, feat)
            pairs.append((row * nfeat + feat, to_row * nfeat + to_feat))
    return lax.ppermute(array, ("row", "feat"), pairs)


def mixed(array, turn):
    def to(row, feat):
        straight = (row + feat) % 2 == 0
        return TURNS[turn if straight else 3 - turn][row], feat if straight else feat ^ 1

    return permute(array, to)


def four_shards(queries, train_rows, inv_gram):
    row, feat = lax.axis_index("row"), lax.axis_index("feat")
    (t_first,) = pack((0,), train_rows)
    t_second, t_third, q_others = pack((1, 2), train_rows, queries, t_first)
    q_pair = swap(q_others, "row", 1)
    cross = send(t_first, "row", lambda i: TURNS[0][i])
    second, third = mixed(t_second, 1), mixed(t_third, 2)
    halves = split_block(cross, SPLIT_COST)
    *prepared, t_mine = prepare(queries, inv_gram, train_rows)
    *conditioned, whole = condition_pair(prepared, q_pair, swap(q_pair, "grp", 1), halves[1])
    other = split_block(swap(whole, "feat", 1), FREE)

    own_core = (row + feat) % 2 == 0
    own, cross = score(conditioned, t_mine), split_score(conditioned, halves, t_mine.shape[0])
    early = jnp.where(own_core, own, cross) + swap(jnp.where(own_core, cross, own), "feat", 1)
    third = split_block(third, SPLIT_COST)
    keep, keep_pair, give, give_pair = last_scores(conditioned, other, second, third, early)
    there = permute(keep_pair, lambda r, f: (r ^ 1, f))
    across = permute(give_pair, lambda r, f: (r ^ 1, f ^ 2))
    beside = permute(give, lambda r, f: (r, f ^ 2))
    return (keep + there + across + beside).T


def solution(mesh):
    four = mesh.shape["row"] == 4 and mesh.shape["feat"] == 4
    return jax.shard_map(
        four_shards if four else any_shards,
        mesh=mesh,
        in_specs=(P("row", "feat"), P(("grp", "row"), "feat"), P("feat", None, None)),
        out_specs=P("row", ("grp", "feat")),
        check_vma=False,
    )
```

```python
import functools

import jax
import jax.numpy as jnp
from jax import lax
from jax.experimental import pallas as pl
from jax.experimental.pallas import tpu as pltpu
from jax.sharding import PartitionSpec as P

HIGHEST = lax.Precision.HIGHEST
ANYWHERE = pl.BlockSpec(memory_space=pl.ANY)
VMEM = pl.BlockSpec(memory_space=pltpu.VMEM)
TURNS = ((3, 2, 1, 0), (1, 0, 3, 2), (2, 3, 0, 1))
FREE = pl.CostEstimate(flops=0, bytes_accessed=0, transcendentals=0)


def send(array, axis, to):
    devices = lax.axis_size(axis)
    return lax.ppermute(array, axis, [(i, to(i)) for i in range(devices)])


def swap(array, axis, bit):
    return send(array, axis, lambda i: i ^ bit)


MID_COST = pl.CostEstimate(flops=1 << 31, bytes_accessed=8 << 20, transcendentals=0)
SPLIT_COST = pl.CostEstimate(flops=8589934592, bytes_accessed=67108864, transcendentals=0)
PREPARE_COST = pl.CostEstimate(flops=1 << 31, bytes_accessed=8 << 20, transcendentals=0)


def condition(queries, inv_gram):
    rows = queries.shape[0]
    nblocks, modsize = inv_gram.shape[0], inv_gram.shape[1]
    blocks = queries.reshape(rows, nblocks, modsize)
    out = jnp.einsum("qbi,bij->qbj", blocks, inv_gram, precision=HIGHEST)
    return out.reshape(rows, nblocks * modsize)


def block_scores(left, right):
    return jnp.dot(left, right.T, precision=HIGHEST, preferred_element_type=jnp.float32)


def any_shards(queries, train_rows, inv_gram):
    qrows, fshard = queries.shape
    trows = train_rows.shape[0]
    nrow, nfeat = lax.axis_size("row"), lax.axis_size("feat")
    row, feat = lax.axis_index("row"), lax.axis_index("feat")
    half, nmod = fshard // 2, inv_gram.shape[0] // 2
    side = row % 2

    def mine(array):
        return lax.dynamic_slice_in_dim(array, side * half, half, 1)

    def others(array):
        return lax.dynamic_slice_in_dim(array, (1 - side) * half, half, 1)

    q_mine, q_others = mine(queries), others(queries)
    t_mine, t_others = mine(train_rows), others(train_rows)
    q_pair = swap(q_others, "row", 1)
    blocks = [(t_mine, row), (swap(t_others, "row", 1), row ^ 1)]
    for step in range(2, nrow, 2):
        blocks.append((send(t_mine, "row", lambda i: (i + step) % nrow), (row - step) % nrow))
        blocks.append((send(t_others, "row", lambda i: ((i + step) % nrow) ^ 1), ((row ^ 1) - step) % nrow))

    gram = lax.dynamic_slice_in_dim(inv_gram, side * nmod, nmod, 0)
    conditioned = condition(jnp.concatenate([q_mine, q_pair], axis=0), gram)
    partial = jnp.zeros((nrow, 2 * qrows, trows), jnp.float32)
    for block, source in blocks:
        partial = lax.dynamic_update_slice(partial, block_scores(conditioned, block)[None], (source, 0, 0))

    left, bit = nfeat, 1
    partial = partial.reshape(nfeat, nrow // nfeat, 2 * qrows, trows)
    while left > 1:
        pairs = partial.reshape(left // 2, 2, *partial.shape[1:])
        odd = (feat // bit) % 2 == 1
        keep = jnp.where(odd, pairs[:, 1], pairs[:, 0])
        give = jnp.where(odd, pairs[:, 0], pairs[:, 1])
        partial = keep + swap(give, "feat", bit)
        left, bit = left // 2, bit * 2
    partial = partial[0]
    scores = partial[:, :qrows] + swap(partial[:, qrows:], "row", 1)
    return scores.transpose(1, 0, 2).reshape(qrows, -1)


def at_row(table):
    row = lax.axis_index("row")
    return sum(jnp.where(row == i, value, 0) for i, value in enumerate(table))


def pack_kernel(*refs, turns, queries):
    outs, sems = refs[-1 - len(turns) - queries : -1], refs[-1]
    t_ref = refs[0]
    half = t_ref.shape[1] // 2

    def columns(which):
        return pl.ds(pl.multiple_of(which * half, half), half)

    other = (lax.axis_index("row") + lax.axis_index("feat")) % 2 != 0
    wanted = [at_row([target % 2 for target in targets]) for targets in TURNS]
    wanted = [wanted[0], jnp.where(other, wanted[2], wanted[1]), jnp.where(other, wanted[1], wanted[2])]
    copies = [(t_ref.at[:, columns(wanted[turn])], out) for turn, out in zip(turns, outs)]
    if queries:
        qrows = outs[-1].shape[0]
        rows = pl.ds(pl.multiple_of(lax.axis_index("grp") * qrows, qrows), qrows)
        copies.append((refs[1].at[rows, columns(1 - lax.axis_index("row") % 2)], outs[-1]))
    copies = [pltpu.make_async_copy(*pair, sems.at[i]) for i, pair in enumerate(copies)]
    for copy in copies:
        copy.start()
    for copy in copies:
        copy.wait()


def pack(turns, train_rows, *rest):
    trows, half = train_rows.shape[0], train_rows.shape[1] // 2
    rows = [trows for _ in turns] + [array.shape[0] // 2 for array in rest[:1]]
    return pl.pallas_call(
        functools.partial(pack_kernel, turns=turns, queries=len(rest[:1])),
        out_shape=[pltpu.VMEM((size, half), jnp.float32) for size in rows],
        in_specs=[ANYWHERE] * (1 + len(rest)),
        out_specs=[VMEM] * len(rows),
        scratch_shapes=[pltpu.SemaphoreType.DMA((len(rows),))],
        cost_estimate=FREE,
    )(train_rows, *rest)


def split(x):
    high = x.astype(jnp.bfloat16)
    return high, (x - high.astype(jnp.float32)).astype(jnp.bfloat16)


def dot3(left, right, dimension_numbers):
    dot = functools.partial(
        lax.dot_general, dimension_numbers=dimension_numbers, preferred_element_type=jnp.float32
    )
    return dot(left[0], right[1]) + dot(left[1], right[0]) + dot(left[0], right[0])


PLAIN = (((1,), (0,)), ((), ()))


def prepare_kernel(q_hbm, gram_hbm, t_hbm, high_ref, low_ref, g_high_ref, g_low_ref, t_ref, q_ref, gram_ref, sems):
    side = lax.axis_index("row") % 2
    nmod, modsize = gram_ref.shape[0], gram_ref.shape[1]
    half = nmod * modsize
    columns = pl.ds(pl.multiple_of(side * half, half), half)
    get_q = pltpu.make_async_copy(q_hbm.at[:, columns], q_ref, sems.at[0])
    get_t = pltpu.make_async_copy(t_hbm.at[:, columns], t_ref, sems.at[2])
    get_gram = pltpu.make_async_copy(gram_hbm.at[pl.ds(side * nmod, nmod)], gram_ref, sems.at[1])
    for copy in (get_q, get_gram, get_t):
        copy.start()
    for copy in (get_q, get_gram, get_t):
        copy.wait()
    for m in range(nmod):
        columns = slice(m * modsize, (m + 1) * modsize)
        gram = split(gram_ref[m])
        g_high_ref[m], g_low_ref[m] = gram
        high_ref[:, columns], low_ref[:, columns] = split(dot3(split(q_ref[:, columns]), gram, PLAIN))


def prepare(queries, inv_gram, train_rows):
    qrows, half = queries.shape[0], queries.shape[1] // 2
    nmod, modsize = inv_gram.shape[0] // 2, inv_gram.shape[1]
    conditioned = pltpu.VMEM((qrows, half), jnp.bfloat16)
    gram = pltpu.VMEM((nmod, modsize, modsize), jnp.bfloat16)
    return pl.pallas_call(
        prepare_kernel,
        out_shape=[conditioned, conditioned, gram, gram, pltpu.VMEM((train_rows.shape[0], half), jnp.float32)],
        in_specs=[ANYWHERE] * 3,
        out_specs=[VMEM] * 5,
        scratch_shapes=[
            pltpu.VMEM((qrows, half), jnp.float32),
            pltpu.VMEM((nmod, modsize, modsize), jnp.float32),
            pltpu.SemaphoreType.DMA((3,)),
        ],
        cost_estimate=PREPARE_COST,
        compiler_params=pltpu.CompilerParams(vmem_limit_bytes=24 << 20),
    )(queries, inv_gram, train_rows)


def condition_kernel(own_high, own_low, g_high, g_low, straight_ref, swapped_ref, after_ref, high_ref, low_ref, whole_ref):
    qrows, modsize = own_high.shape[0], g_high.shape[1]
    first = lax.axis_index("grp") == 0
    high_ref[:qrows], low_ref[:qrows] = own_high[...], own_low[...]
    for m in range(g_high.shape[0]):
        columns = slice(m * modsize, (m + 1) * modsize)
        straight, swapped = straight_ref[:, columns], swapped_ref[:, columns]
        pair = [jnp.where(first, straight, swapped), jnp.where(first, swapped, straight)]
        out = dot3(split(jnp.concatenate(pair, axis=0)), (g_high[m], g_low[m]), PLAIN)
        high_ref[qrows:, columns], low_ref[qrows:, columns] = split(out)
    whole_ref[...] = high_ref[...].astype(jnp.float32) + low_ref[...].astype(jnp.float32)


def condition_pair(prepared, straight, swapped, after):
    out = jax.ShapeDtypeStruct((4 * straight.shape[0], straight.shape[1]), jnp.bfloat16)
    return pl.pallas_call(
        condition_kernel,
        out_shape=[out, out, jax.ShapeDtypeStruct(out.shape, jnp.float32)],
        in_specs=[VMEM] * 6 + [ANYWHERE],
        out_specs=[VMEM] * 3,
        cost_estimate=FREE,
        compiler_params=pltpu.CompilerParams(vmem_limit_bytes=24 << 20),
    )(*prepared, straight, swapped, after)


def split_rows(block):
    rows = block.shape[0]
    if rows % 16:
        block = jnp.concatenate([block, jnp.zeros((-rows % 16, block.shape[1]), block.dtype)], axis=0)
    return split(block)


def split_scores_of(high, low, t_high, t_low):
    rows = t_high.shape[0]
    dot = functools.partial(
        lax.dot_general, dimension_numbers=(((1,), (1,)), ((), ())), preferred_element_type=jnp.float32
    )
    both = dot(jnp.concatenate([t_high, t_low], axis=0), high)
    return both[rows:] + dot(t_high, low) + both[:rows]


def scores_kernel(high_ref, low_ref, t_ref, out_ref):
    out_ref[...] = split_scores_of(high_ref[...], low_ref[...], *split_rows(t_ref[...]))[: out_ref.shape[0]]


def score(conditioned, block):
    return pl.pallas_call(
        scores_kernel,
        out_shape=jax.ShapeDtypeStruct((block.shape[0], conditioned[0].shape[0]), jnp.float32),
        in_specs=[VMEM] * 3,
        out_specs=VMEM,
        cost_estimate=FREE,
        compiler_params=pltpu.CompilerParams(vmem_limit_bytes=16 << 20),
    )(*conditioned, block)


def last_kernel(*refs):
    mine, other, second_ref, third = refs[:2], refs[2:4], refs[4], refs[5:7]
    early_ref, late_ref = refs[7], refs[12]
    row, feat = lax.axis_index("row"), lax.axis_index("feat")
    here = feat % 2 == row % 2

    def scores(left, right):
        left, right = [ref[...] for ref in left], [ref[...] for ref in right]
        total = split_scores_of(*left, *[ref[...] for ref in third])
        return (total + split_scores_of(*right, *split_rows(second_ref[...])))[: late_ref.shape[0]]

    @pl.when(here)
    def _():
        late_ref[...] = scores(mine, other)

    @pl.when(jnp.logical_not(here))
    def _():
        late_ref[...] = scores(other, mine)

    late, early = late_ref[...], early_ref[...]
    own = (row + feat + row // 2 + feat // 2) % 2 != 0
    qrows = early.shape[1] // 2
    keep, give = jnp.where(own, late, early), jnp.where(own, early, late)
    refs[8][...], refs[9][...] = keep[:, :qrows], keep[:, qrows:]
    refs[10][...], refs[11][...] = give[:, :qrows], give[:, qrows:]


def last_scores(mine, other, second, third, early):
    trows, queries = early.shape
    out = jax.ShapeDtypeStruct((trows, queries // 2), jnp.float32)
    return pl.pallas_call(
        last_kernel,
        out_shape=[out] * 4,
        in_specs=[VMEM] * 8,
        out_specs=[VMEM] * 4,
        scratch_shapes=[pltpu.VMEM((trows, queries), jnp.float32)],
        cost_estimate=FREE,
        compiler_params=pltpu.CompilerParams(vmem_limit_bytes=16 << 20),
    )(*mine, *other, second, *third, early)


def split_kernel(given_ref, high_ref, low_ref):
    high_ref[...], low_ref[...] = split_rows(given_ref[...])


def split_block(block, cost):
    rows, columns = block.shape
    out = jax.ShapeDtypeStruct((rows + -rows % 16, columns), jnp.bfloat16)
    return pl.pallas_call(
        split_kernel,
        out_shape=[out, out],
        in_specs=[VMEM],
        out_specs=[VMEM] * 2,
        cost_estimate=cost,
        compiler_params=pltpu.CompilerParams(vmem_limit_bytes=16 << 20),
    )(block)


def split_scores_kernel(high_ref, low_ref, t_high_ref, t_low_ref, out_ref):
    out = split_scores_of(high_ref[...], low_ref[...], t_high_ref[...], t_low_ref[...])
    out_ref[...] = out[: out_ref.shape[0]]


def split_score(conditioned, halves, trows):
    return pl.pallas_call(
        split_scores_kernel,
        out_shape=jax.ShapeDtypeStruct((trows, conditioned[0].shape[0]), jnp.float32),
        in_specs=[VMEM] * 4,
        out_specs=VMEM,
        cost_estimate=FREE,
        compiler_params=pltpu.CompilerParams(vmem_limit_bytes=16 << 20),
    )(*conditioned, *halves)


def permute(array, to):
    nrow, nfeat = lax.axis_size("row"), lax.axis_size("feat")
    pairs = []
    for row in range(nrow):
        for feat in range(nfeat):
            to_row, to_feat = to(row, feat)
            pairs.append((row * nfeat + feat, to_row * nfeat + to_feat))
    return lax.ppermute(array, ("row", "feat"), pairs)


def mixed(array, turn):
    def to(row, feat):
        straight = (row + feat) % 2 == 0
        return TURNS[turn if straight else 3 - turn][row], feat if straight else feat ^ 1

    return permute(array, to)


def four_shards(queries, train_rows, inv_gram):
    row, feat = lax.axis_index("row"), lax.axis_index("feat")
    (t_first,) = pack((0,), train_rows)
    t_second, t_third, q_others = pack((1, 2), train_rows, queries, t_first)
    q_pair = swap(q_others, "row", 1)
    cross = send(t_first, "row", lambda i: TURNS[0][i])
    second, third = mixed(t_second, 1), mixed(t_third, 2)
    halves = split_block(cross, SPLIT_COST)
    *prepared, t_mine = prepare(queries, inv_gram, train_rows)
    *conditioned, whole = condition_pair(prepared, q_pair, swap(q_pair, "grp", 1), halves[1])
    other = split_block(swap(whole, "feat", 1), FREE)

    own_core = (row + feat) % 2 == 0
    own, cross = score(conditioned, t_mine), split_score(conditioned, halves, t_mine.shape[0])
    early = jnp.where(own_core, own, cross) + swap(jnp.where(own_core, cross, own), "feat", 1)
    third = split_block(third, SPLIT_COST)
    keep, keep_pair, give, give_pair = last_scores(conditioned, other, second, third, early)
    there = permute(keep_pair, lambda r, f: (r ^ 1, f))
    across = permute(give_pair, lambda r, f: (r ^ 1, f ^ 2))
    beside = permute(give, lambda r, f: (r, f ^ 2))
    return (keep + there + across + beside).T


def solution(mesh):
    four = mesh.shape["row"] == 4 and mesh.shape["feat"] == 4
    return jax.shard_map(
        four_shards if four else any_shards,
        mesh=mesh,
        in_specs=(P("row", "feat"), P(("grp", "row"), "feat"), P("feat", None, None)),
        out_specs=P("row", ("grp", "feat")),
        check_vma=False,
    )
```

```python
import functools

import jax
import jax.numpy as jnp
from jax import lax
from jax.experimental import pallas as pl
from jax.experimental.pallas import tpu as pltpu
from jax.sharding import PartitionSpec as P

HIGHEST = lax.Precision.HIGHEST
ANYWHERE = pl.BlockSpec(memory_space=pl.ANY)
VMEM = pl.BlockSpec(memory_space=pltpu.VMEM)
TURNS = ((3, 2, 1, 0), (1, 0, 3, 2), (2, 3, 0, 1))
FREE = pl.CostEstimate(flops=0, bytes_accessed=0, transcendentals=0)


def send(array, axis, to):
    devices = lax.axis_size(axis)
    return lax.ppermute(array, axis, [(i, to(i)) for i in range(devices)])


def swap(array, axis, bit):
    return send(array, axis, lambda i: i ^ bit)


MID_COST = pl.CostEstimate(flops=1 << 31, bytes_accessed=8 << 20, transcendentals=0)
SPLIT_COST = pl.CostEstimate(flops=8589934592, bytes_accessed=67108864, transcendentals=0)
PREPARE_COST = pl.CostEstimate(flops=1 << 31, bytes_accessed=8 << 20, transcendentals=0)


def condition(queries, inv_gram):
    rows = queries.shape[0]
    nblocks, modsize = inv_gram.shape[0], inv_gram.shape[1]
    blocks = queries.reshape(rows, nblocks, modsize)
    out = jnp.einsum("qbi,bij->qbj", blocks, inv_gram, precision=HIGHEST)
    return out.reshape(rows, nblocks * modsize)


def block_scores(left, right):
    return jnp.dot(left, right.T, precision=HIGHEST, preferred_element_type=jnp.float32)


def any_shards(queries, train_rows, inv_gram):
    qrows, fshard = queries.shape
    trows = train_rows.shape[0]
    nrow, nfeat = lax.axis_size("row"), lax.axis_size("feat")
    row, feat = lax.axis_index("row"), lax.axis_index("feat")
    half, nmod = fshard // 2, inv_gram.shape[0] // 2
    side = row % 2

    def mine(array):
        return lax.dynamic_slice_in_dim(array, side * half, half, 1)

    def others(array):
        return lax.dynamic_slice_in_dim(array, (1 - side) * half, half, 1)

    q_mine, q_others = mine(queries), others(queries)
    t_mine, t_others = mine(train_rows), others(train_rows)
    q_pair = swap(q_others, "row", 1)
    blocks = [(t_mine, row), (swap(t_others, "row", 1), row ^ 1)]
    for step in range(2, nrow, 2):
        blocks.append((send(t_mine, "row", lambda i: (i + step) % nrow), (row - step) % nrow))
        blocks.append((send(t_others, "row", lambda i: ((i + step) % nrow) ^ 1), ((row ^ 1) - step) % nrow))

    gram = lax.dynamic_slice_in_dim(inv_gram, side * nmod, nmod, 0)
    conditioned = condition(jnp.concatenate([q_mine, q_pair], axis=0), gram)
    partial = jnp.zeros((nrow, 2 * qrows, trows), jnp.float32)
    for block, source in blocks:
        partial = lax.dynamic_update_slice(partial, block_scores(conditioned, block)[None], (source, 0, 0))

    left, bit = nfeat, 1
    partial = partial.reshape(nfeat, nrow // nfeat, 2 * qrows, trows)
    while left > 1:
        pairs = partial.reshape(left // 2, 2, *partial.shape[1:])
        odd = (feat // bit) % 2 == 1
        keep = jnp.where(odd, pairs[:, 1], pairs[:, 0])
        give = jnp.where(odd, pairs[:, 0], pairs[:, 1])
        partial = keep + swap(give, "feat", bit)
        left, bit = left // 2, bit * 2
    partial = partial[0]
    scores = partial[:, :qrows] + swap(partial[:, qrows:], "row", 1)
    return scores.transpose(1, 0, 2).reshape(qrows, -1)


def at_row(table):
    row = lax.axis_index("row")
    return sum(jnp.where(row == i, value, 0) for i, value in enumerate(table))


def pack_kernel(*refs, turns, queries):
    outs, sems = refs[-1 - len(turns) - queries : -1], refs[-1]
    t_ref = refs[0]
    half = t_ref.shape[1] // 2

    def columns(which):
        return pl.ds(pl.multiple_of(which * half, half), half)

    other = (lax.axis_index("row") + lax.axis_index("feat")) % 2 != 0
    wanted = [at_row([target % 2 for target in targets]) for targets in TURNS]
    wanted = [wanted[0], jnp.where(other, wanted[2], wanted[1]), jnp.where(other, wanted[1], wanted[2])]
    copies = [(t_ref.at[:, columns(wanted[turn])], out) for turn, out in zip(turns, outs)]
    if queries:
        qrows = outs[-1].shape[0]
        rows = pl.ds(pl.multiple_of(lax.axis_index("grp") * qrows, qrows), qrows)
        copies.append((refs[1].at[rows, columns(1 - lax.axis_index("row") % 2)], outs[-1]))
    copies = [pltpu.make_async_copy(*pair, sems.at[i]) for i, pair in enumerate(copies)]
    for copy in copies:
        copy.start()
    for copy in copies:
        copy.wait()


def pack(turns, train_rows, *rest):
    trows, half = train_rows.shape[0], train_rows.shape[1] // 2
    rows = [trows for _ in turns] + [array.shape[0] // 2 for array in rest[:1]]
    return pl.pallas_call(
        functools.partial(pack_kernel, turns=turns, queries=len(rest[:1])),
        out_shape=[pltpu.VMEM((size, half), jnp.float32) for size in rows],
        in_specs=[ANYWHERE] * (1 + len(rest)),
        out_specs=[VMEM] * len(rows),
        scratch_shapes=[pltpu.SemaphoreType.DMA((len(rows),))],
        cost_estimate=FREE,
    )(train_rows, *rest)


def split(x):
    high = x.astype(jnp.bfloat16)
    return high, (x - high.astype(jnp.float32)).astype(jnp.bfloat16)


def dot3(left, right, dimension_numbers):
    dot = functools.partial(
        lax.dot_general, dimension_numbers=dimension_numbers, preferred_element_type=jnp.float32
    )
    return dot(left[0], right[1]) + dot(left[1], right[0]) + dot(left[0], right[0])


PLAIN = (((1,), (0,)), ((), ()))


def prepare_kernel(q_hbm, gram_hbm, t_hbm, high_ref, low_ref, g_high_ref, g_low_ref, t_ref, q_ref, gram_ref, sems):
    side = lax.axis_index("row") % 2
    nmod, modsize = gram_ref.shape[0], gram_ref.shape[1]
    half = nmod * modsize
    columns = pl.ds(pl.multiple_of(side * half, half), half)
    get_q = pltpu.make_async_copy(q_hbm.at[:, columns], q_ref, sems.at[0])
    get_t = pltpu.make_async_copy(t_hbm.at[:, columns], t_ref, sems.at[2])
    get_gram = pltpu.make_async_copy(gram_hbm.at[pl.ds(side * nmod, nmod)], gram_ref, sems.at[1])
    for copy in (get_q, get_gram, get_t):
        copy.start()
    for copy in (get_q, get_gram, get_t):
        copy.wait()
    for m in range(nmod):
        columns = slice(m * modsize, (m + 1) * modsize)
        gram = split(gram_ref[m])
        g_high_ref[m], g_low_ref[m] = gram
        high_ref[:, columns], low_ref[:, columns] = split(dot3(split(q_ref[:, columns]), gram, PLAIN))


def prepare(queries, inv_gram, train_rows):
    qrows, half = queries.shape[0], queries.shape[1] // 2
    nmod, modsize = inv_gram.shape[0] // 2, inv_gram.shape[1]
    conditioned = pltpu.VMEM((qrows, half), jnp.bfloat16)
    gram = pltpu.VMEM((nmod, modsize, modsize), jnp.bfloat16)
    return pl.pallas_call(
        prepare_kernel,
        out_shape=[conditioned, conditioned, gram, gram, pltpu.VMEM((train_rows.shape[0], half), jnp.float32)],
        in_specs=[ANYWHERE] * 3,
        out_specs=[VMEM] * 5,
        scratch_shapes=[
            pltpu.VMEM((qrows, half), jnp.float32),
            pltpu.VMEM((nmod, modsize, modsize), jnp.float32),
            pltpu.SemaphoreType.DMA((3,)),
        ],
        cost_estimate=PREPARE_COST,
        compiler_params=pltpu.CompilerParams(vmem_limit_bytes=24 << 20),
    )(queries, inv_gram, train_rows)


def condition_kernel(own_high, own_low, g_high, g_low, straight_ref, swapped_ref, after_ref, high_ref, low_ref, whole_ref):
    qrows, modsize = own_high.shape[0], g_high.shape[1]
    first = lax.axis_index("grp") == 0
    high_ref[:qrows], low_ref[:qrows] = own_high[...], own_low[...]
    for m in range(g_high.shape[0]):
        columns = slice(m * modsize, (m + 1) * modsize)
        straight, swapped = straight_ref[:, columns], swapped_ref[:, columns]
        pair = [jnp.where(first, straight, swapped), jnp.where(first, swapped, straight)]
        out = dot3(split(jnp.concatenate(pair, axis=0)), (g_high[m], g_low[m]), PLAIN)
        high_ref[qrows:, columns], low_ref[qrows:, columns] = split(out)
    whole_ref[...] = high_ref[...].astype(jnp.float32) + low_ref[...].astype(jnp.float32)


def condition_pair(prepared, straight, swapped, after):
    out = jax.ShapeDtypeStruct((4 * straight.shape[0], straight.shape[1]), jnp.bfloat16)
    return pl.pallas_call(
        condition_kernel,
        out_shape=[out, out, jax.ShapeDtypeStruct(out.shape, jnp.float32)],
        in_specs=[VMEM] * 6 + [ANYWHERE],
        out_specs=[VMEM] * 3,
        cost_estimate=FREE,
        compiler_params=pltpu.CompilerParams(vmem_limit_bytes=24 << 20),
    )(*prepared, straight, swapped, after)


def split_rows(block):
    rows = block.shape[0]
    if rows % 16:
        block = jnp.concatenate([block, jnp.zeros((-rows % 16, block.shape[1]), block.dtype)], axis=0)
    return split(block)


def split_scores_of(high, low, t_high, t_low):
    rows = t_high.shape[0]
    dot = functools.partial(
        lax.dot_general, dimension_numbers=(((1,), (1,)), ((), ())), preferred_element_type=jnp.float32
    )
    both = dot(jnp.concatenate([t_high, t_low], axis=0), high)
    return both[rows:] + dot(t_high, low) + both[:rows]


def scores_kernel(high_ref, low_ref, t_ref, out_ref):
    out_ref[...] = split_scores_of(high_ref[...], low_ref[...], *split_rows(t_ref[...]))[: out_ref.shape[0]]


def score(conditioned, block):
    return pl.pallas_call(
        scores_kernel,
        out_shape=jax.ShapeDtypeStruct((block.shape[0], conditioned[0].shape[0]), jnp.float32),
        in_specs=[VMEM] * 3,
        out_specs=VMEM,
        cost_estimate=FREE,
        compiler_params=pltpu.CompilerParams(vmem_limit_bytes=16 << 20),
    )(*conditioned, block)


def last_kernel(*refs):
    mine, other, second_ref, third = refs[:2], refs[2:4], refs[4], refs[5:7]
    early_ref, late_ref = refs[7], refs[12]
    row, feat = lax.axis_index("row"), lax.axis_index("feat")
    here = feat % 2 == row % 2

    def scores(left, right):
        left, right = [ref[...] for ref in left], [ref[...] for ref in right]
        total = split_scores_of(*left, *[ref[...] for ref in third])
        return (total + split_scores_of(*right, *split_rows(second_ref[...])))[: late_ref.shape[0]]

    @pl.when(here)
    def _():
        late_ref[...] = scores(mine, other)

    @pl.when(jnp.logical_not(here))
    def _():
        late_ref[...] = scores(other, mine)

    late, early = late_ref[...], early_ref[...]
    own = (row + feat + row // 2 + feat // 2) % 2 != 0
    qrows = early.shape[1] // 2
    keep, give = jnp.where(own, late, early), jnp.where(own, early, late)
    refs[8][...], refs[9][...] = keep[:, :qrows], keep[:, qrows:]
    refs[10][...], refs[11][...] = give[:, :qrows], give[:, qrows:]


def last_scores(mine, other, second, third, early):
    trows, queries = early.shape
    out = jax.ShapeDtypeStruct((trows, queries // 2), jnp.float32)
    return pl.pallas_call(
        last_kernel,
        out_shape=[out] * 4,
        in_specs=[VMEM] * 8,
        out_specs=[VMEM] * 4,
        scratch_shapes=[pltpu.VMEM((trows, queries), jnp.float32)],
        cost_estimate=FREE,
        compiler_params=pltpu.CompilerParams(vmem_limit_bytes=16 << 20),
    )(*mine, *other, second, *third, early)


def split_kernel(given_ref, high_ref, low_ref):
    high_ref[...], low_ref[...] = split_rows(given_ref[...])


def split_block(block, cost):
    rows, columns = block.shape
    out = jax.ShapeDtypeStruct((rows + -rows % 16, columns), jnp.bfloat16)
    return pl.pallas_call(
        split_kernel,
        out_shape=[out, out],
        in_specs=[VMEM],
        out_specs=[VMEM] * 2,
        cost_estimate=cost,
        compiler_params=pltpu.CompilerParams(vmem_limit_bytes=16 << 20),
    )(block)


def split_scores_kernel(high_ref, low_ref, t_high_ref, t_low_ref, out_ref):
    out = split_scores_of(high_ref[...], low_ref[...], t_high_ref[...], t_low_ref[...])
    out_ref[...] = out[: out_ref.shape[0]]


def split_score(conditioned, halves, trows):
    return pl.pallas_call(
        split_scores_kernel,
        out_shape=jax.ShapeDtypeStruct((trows, conditioned[0].shape[0]), jnp.float32),
        in_specs=[VMEM] * 4,
        out_specs=VMEM,
        cost_estimate=FREE,
        compiler_params=pltpu.CompilerParams(vmem_limit_bytes=16 << 20),
    )(*conditioned, *halves)


def permute(array, to):
    nrow, nfeat = lax.axis_size("row"), lax.axis_size("feat")
    pairs = []
    for row in range(nrow):
        for feat in range(nfeat):
            to_row, to_feat = to(row, feat)
            pairs.append((row * nfeat + feat, to_row * nfeat + to_feat))
    return lax.ppermute(array, ("row", "feat"), pairs)


def mixed(array, turn):
    def to(row, feat):
        straight = (row + feat) % 2 == 0
        return TURNS[turn if straight else 3 - turn][row], feat if straight else feat ^ 1

    return permute(array, to)


def four_shards(queries, train_rows, inv_gram):
    row, feat = lax.axis_index("row"), lax.axis_index("feat")
    (t_first,) = pack((0,), train_rows)
    t_second, t_third, q_others = pack((1, 2), train_rows, queries, t_first)
    q_pair = swap(q_others, "row", 1)
    cross = send(t_first, "row", lambda i: TURNS[0][i])
    second, third = mixed(t_second, 1), mixed(t_third, 2)
    halves = split_block(cross, SPLIT_COST)
    *prepared, t_mine = prepare(queries, inv_gram, train_rows)
    *conditioned, whole = condition_pair(prepared, q_pair, swap(q_pair, "grp", 1), halves[1])
    other = split_block(swap(whole, "feat", 1), FREE)

    own_core = (row + feat) % 2 == 0
    own, cross = score(conditioned, t_mine), split_score(conditioned, halves, t_mine.shape[0])
    early = jnp.where(own_core, own, cross) + swap(jnp.where(own_core, cross, own), "feat", 1)
    third = split_block(third, SPLIT_COST)
    keep, keep_pair, give, give_pair = last_scores(conditioned, other, second, third, early)
    across = permute(give_pair, lambda r, f: (r ^ 1, f ^ 2))
    beside = permute(give, lambda r, f: (r, f ^ 2))
    there = permute(keep_pair, lambda r, f: (r ^ 1, f))
    return (keep + across + beside + there).T


def solution(mesh):
    four = mesh.shape["row"] == 4 and mesh.shape["feat"] == 4
    return jax.shard_map(
        four_shards if four else any_shards,
        mesh=mesh,
        in_specs=(P("row", "feat"), P(("grp", "row"), "feat"), P("feat", None, None)),
        out_specs=P("row", ("grp", "feat")),
        check_vma=False,
    )
```
